512 devices in a mesh: dp: 32 (over x, y), tensor: 16 (over z, core).
Axes of the slice: x: 4, y: 8, z: 8, core: 2. Of those that a mesh axis runs over, the one named last changes fastest.
Arguments:
- hidden: bfloat16 [65536, 8192], P('dp', 'tensor'), may hold values from -6 to 6
- value_matrix: bfloat16 [8192, 1024], P('tensor'), may hold values from -0.09375 to 0.09375
- adapter_down_store: bfloat16 [64, 8192, 64], P('dp', 'tensor'), may hold values from -0.0625 to 0.0625
- adapter_up_store: bfloat16 [64, 64, 1024], P('dp', None, 'tensor'), may hold values from -0.75 to 0.75
- adapter_slot: int32 [64], replicated, may hold values from 0 to 63, each once
- rollout_adapter: int32 [128], P('dp'), may hold values from 0 to 63
- lengths: int32 [128], P('dp'), may hold values from 128 to 512, as said below
Outputs:
- values: bfloat16 [65536, 1024], P('dp', 'tensor')
The draws below stay inside these ranges and needn't reach their ends.
Inputs may be any that keep to these rules, and one draw needn't show every extreme that they name: `adapter_slot`: each slot once. `lengths`: in every draw some rollout has exactly 512 valid tokens and some exactly a quarter of 512.
All inputs are finite; a program needn't handle non-finite values.
Results may differ from the reference program's by a relative error of at most 0.024.
Values may be sent and summed in bfloat16 or wider, within the bound.
No kernel may reach another device: no remote copies, remote signals or barrier semaphores. Data moves between devices by JAX's collectives and lax.ppermute only.
A program may use at most 64 MiB of HBM per device.

```python
import math
import jax
import jax.numpy as jnp
import numpy as np
from jax import lax

MODEL_WIDTH = 8192
VALUE_WIDTH = 1024
ADAPTER_RANK = 64
ADAPTER_TOTAL = 64
ROLL_LEN = 512
ROLLOUTS = 128
TOKENS = 65536
N_TENSOR = 16


def draw_lengths(key, part):
    key = jax.random.fold_in(key, 11)
    key_values, key_index = jax.random.split(key)
    lengths_drawn = jax.random.randint(key_values, (ROLLOUTS,), ROLL_LEN // 4, ROLL_LEN + 1)
    longest = jax.random.randint(key_index, (), 0, ROLLOUTS)
    shortest = (longest + 1) % ROLLOUTS
    positions = jnp.arange(ROLLOUTS)
    lengths_drawn = jnp.where(positions == longest, ROLL_LEN, lengths_drawn)
    lengths_drawn = jnp.where(positions == shortest, ROLL_LEN // 4, lengths_drawn)
    return lengths_drawn.astype(jnp.int32)


def place_ends(values, own_key, smallest, top_value):
    longest = values.shape.index(max(values.shape))
    spots = []
    for shift in (0, 1):
        where = [jax.random.randint(jax.random.fold_in(own_key, axis), (), 0, length) for axis, length in enumerate(values.shape)]
        where[longest] = (where[longest] + shift) % values.shape[longest]
        spots.append(tuple(where))
    return values.at[spots[0]].set(smallest).at[spots[1]].set(top_value)


def spiked(entries, key, source, target, parts, factor):
    def block_of(dim):
        return (jnp.arange(entries.shape[dim]) // (entries.shape[dim] // parts)).reshape((-1,) + (1,) * (entries.ndim - 1 - dim))

    near = jax.random.permutation(key, parts)[block_of(target)]
    second = (block_of(target) + parts // 2) % parts
    return jnp.where((block_of(source) == near) | (block_of(source) == second), factor * entries, entries)


def block_levels(stream_key, dims, cuts, low, top_value):
    gain, own = 1.0, jax.random.fold_in(stream_key, 6)
    for axis_at, parts in cuts:
        heights = jnp.exp(jax.random.uniform(jax.random.fold_in(own, axis_at), (parts,), jnp.float32, low / len(cuts), top_value / len(cuts)))
        gain = gain * jnp.repeat(heights, dims[axis_at] // parts).reshape([-1 if axis == axis_at else 1 for axis in range(len(dims))])
    return gain


def rank_bounds(count, lean):
    portions = [(1 << 20) // math.isqrt(rank ** lean) + 1 for rank in range(1, count + 1)]
    deviation = 1 + sum(portions) // (1 << 30)
    return np.cumsum(np.array([max(1, weight // deviation) for weight in portions]))


def ranked_ids(stream_key, extent, amount, lean):
    table = rank_bounds(amount, lean)
    ticket = jax.random.randint(jax.random.fold_in(stream_key, 1), extent, 0, int(table[amount - 1]))
    rank = jnp.searchsorted(jnp.asarray(table, jnp.int32), ticket, side="right")
    return jax.random.permutation(jax.random.fold_in(stream_key, 2), amount)[rank].astype(jnp.int32)


def noise(key, extent, spread, reach, cuts=(), kind=jnp.bfloat16):
    values = spread * jax.random.normal(key, extent, jnp.float32)
    if cuts:
        values = values * block_levels(key, extent, cuts, -0.22, 0.18)
    return jnp.clip(values, -reach, reach).astype(kind)


def bell_draw_with(stream_key, dims, spread, most, pieces, heavy, held_as=jnp.bfloat16):
    values = spread * jax.random.normal(stream_key, dims, jnp.float32)
    if pieces:
        values = values * block_levels(stream_key, dims, pieces, -0.22, 0.18)
    return jnp.clip(spiked(values, jax.random.fold_in(stream_key, 3), *heavy), -most, most).astype(held_as)


def setup_inputs(seed: int = 0) -> dict:
    arg_keys = jax.random.split(jax.random.key(seed), 8)
    return {
        "hidden": noise(arg_keys[0], (TOKENS, MODEL_WIDTH), 1.0, 6.0, ((0, 32), (1, 16))),
        "value_matrix": bell_draw_with(arg_keys[1], (MODEL_WIDTH, VALUE_WIDTH), MODEL_WIDTH ** -0.5, 0.09375, ((0, 16),), (0, 1, 16, 2.0)),
        "adapter_down_store": noise(arg_keys[2], (ADAPTER_TOTAL, MODEL_WIDTH, ADAPTER_RANK), MODEL_WIDTH ** -0.5, 0.0625, ((0, 32), (1, 16))),
        "adapter_up_store": noise(arg_keys[3], (ADAPTER_TOTAL, ADAPTER_RANK, VALUE_WIDTH), ADAPTER_RANK ** -0.5, 0.75, ((0, 32), (2, 16))),
        "adapter_slot": jax.random.permutation(arg_keys[4], ADAPTER_TOTAL).astype(jnp.int32),
        "rollout_adapter": place_ends(ranked_ids(arg_keys[5], (ROLLOUTS,), ADAPTER_TOTAL, 2), jax.random.fold_in(arg_keys[5], 3), 0, ADAPTER_TOTAL - 1).astype(jnp.int32),
        "lengths": draw_lengths(jax.random.fold_in(arg_keys[7], 71), 0),
    }


ADAPTER_SCALE = 2.0


def reference(hidden, value_matrix, adapter_down_store, adapter_up_store, adapter_slot, rollout_adapter, lengths):
    block_size = MODEL_WIDTH // N_TENSOR
    slot_index = adapter_slot[rollout_adapter].astype(jnp.int32)
    token_rows = hidden.reshape(ROLLOUTS, ROLL_LEN, MODEL_WIDTH)

    def score_rollout(inputs):
        rollout_rows, picked_slot, valid_count = inputs
        down_matrix = adapter_down_store[picked_slot]
        base_output = jnp.zeros((ROLL_LEN, VALUE_WIDTH), jnp.float32)
        down_sum = jnp.zeros((ROLL_LEN, ADAPTER_RANK), jnp.float32)
        for shard_index in range(N_TENSOR):
            lower = shard_index * block_size
            upper = lower + block_size
            partial_value = jnp.dot(rollout_rows[:, lower:upper], value_matrix[lower:upper], preferred_element_type=jnp.float32)
            base_output = base_output + lax.optimization_barrier(partial_value.astype(jnp.bfloat16)).astype(jnp.float32)
            down_part = jnp.dot(rollout_rows[:, lower:upper], down_matrix[lower:upper], preferred_element_type=jnp.float32)
            down_sum = down_sum + lax.optimization_barrier(down_part.astype(jnp.bfloat16)).astype(jnp.float32)
        down_projected = down_sum.astype(jnp.bfloat16)
        adapter_update = jnp.dot(down_projected, adapter_up_store[picked_slot], preferred_element_type=jnp.float32)
        positions = jnp.arange(ROLL_LEN, dtype=jnp.int32)
        validity_mask = (positions < valid_count)[:, None]
        return jnp.where(validity_mask, base_output + ADAPTER_SCALE * adapter_update, jnp.float32(0.0)).astype(jnp.bfloat16)

    scored_output = lax.map(score_rollout, (token_rows, slot_index, lengths))
    return scored_output.reshape(TOKENS, VALUE_WIDTH)
```

```python
import functools

import jax
import jax.numpy as jnp
from jax import lax
from jax.experimental import pallas as pl
from jax.experimental.pallas import tpu as pltpu
from jax.sharding import Mesh
from jax.sharding import PartitionSpec as P

ADAPTER_SCALE = 2.0
X, CORES = 4, 2
DP, TENSOR = ("x", "y"), ("z", "core")
LANES = 128
KERNEL_VMEM = 8 << 20
PROJECT_VMEM = 32 << 20
PROJECT_CHIPS, PROJECT_ROWS = 4, 1024
NO_COST = pl.CostEstimate(flops=0, bytes_accessed=0, transcendentals=0)


def pick_kernel(index_ref, store_ref, out_ref, sems):
    copies = [
        pltpu.make_async_copy(store_ref.at[index_ref[i]], out_ref.at[i], sems.at[i])
        for i in range(out_ref.shape[0])
    ]
    for copy in copies:
        copy.start()
    for copy in copies:
        copy.wait()


def pick(store, index):
    count = index.shape[0]
    out = jax.ShapeDtypeStruct((count, *store.shape[1:]), store.dtype)
    size = out.size * out.dtype.itemsize
    return pl.pallas_call(
        pick_kernel,
        out_shape=out,
        in_specs=[pl.BlockSpec(memory_space=pltpu.SMEM), pl.BlockSpec(memory_space=pl.ANY)],
        out_specs=pl.BlockSpec(memory_space=pltpu.VMEM),
        scratch_shapes=[pltpu.SemaphoreType.DMA((count,))],
        cost_estimate=pl.CostEstimate(flops=0, bytes_accessed=2 * size, transcendentals=0),
        compiler_params=pltpu.CompilerParams(vmem_limit_bytes=KERNEL_VMEM),
        name="pick_slots",
    )(index, store)


def down_kernel(chunk, index_ref, hidden_ref, factor_ref, out_ref):
    product = lax.dot_general(
        hidden_ref[...],
        factor_ref[0],
        (((1,), (1,)), ((), ())),
        preferred_element_type=jnp.float32,
    ).T.astype(out_ref.dtype)
    for i in range(out_ref.shape[0]):
        out_ref[i] = product[:, i * chunk : (i + 1) * chunk]


def down_projection(hidden, factors, index, members):
    tokens, features = hidden.shape
    _, rank, _ = factors.shape
    count = index.shape[0]
    length, chunk = tokens // count, tokens // members
    per = length // chunk
    return pl.pallas_call(
        functools.partial(down_kernel, chunk),
        grid_spec=pltpu.PrefetchScalarGridSpec(
            num_scalar_prefetch=1,
            grid=(count,),
            in_specs=[
                pl.BlockSpec((length, features), lambda r, index: (r, 0)),
                pl.BlockSpec((1, rank, features), lambda r, index: (index[r], 0, 0)),
            ],
            out_specs=pl.BlockSpec((per, rank, chunk), lambda r, index: (r, 0, 0)),
        ),
        out_shape=jax.ShapeDtypeStruct((members, rank, chunk), hidden.dtype),
        cost_estimate=pl.CostEstimate(
            flops=2 * tokens * features * rank,
            bytes_accessed=2 * (hidden.size + count * rank * features + tokens * rank),
            transcendentals=0,
        ),
        compiler_params=pltpu.CompilerParams(vmem_limit_bytes=KERNEL_VMEM),
        name="down_projection",
    )(index, hidden, factors)


def final_kernel(slots_ref, lengths_ref, base_ref, down_ref, up_ref, out_ref):
    r = pl.program_id(0)
    columns, length = base_ref.shape
    down = jnp.concatenate([down_ref[i] for i in range(down_ref.shape[0])], axis=1)
    update = lax.dot_general(
        up_ref[0, :, :columns],
        down,
        (((0,), (0,)), ((), ())),
        preferred_element_type=jnp.float32,
    )
    total = base_ref[...].astype(jnp.float32) + ADAPTER_SCALE * update
    position = lax.broadcasted_iota(jnp.int32, (columns, length), 1)
    out_ref[...] = jnp.where(position < lengths_ref[r], total, 0.0).astype(out_ref.dtype)


def final(slots, lengths, base, down, up_store):
    columns, tokens = base.shape
    _, rank, width = up_store.shape
    count = slots.shape[0]
    members, _, chunk = down.shape
    per = members // count
    length = tokens // count
    return pl.pallas_call(
        final_kernel,
        grid_spec=pltpu.PrefetchScalarGridSpec(
            num_scalar_prefetch=2,
            grid=(count,),
            in_specs=[
                pl.BlockSpec((columns, length), lambda r, slots, lengths: (0, r)),
                pl.BlockSpec((per, rank, chunk), lambda r, slots, lengths: (r, 0, 0)),
                pl.BlockSpec((1, rank, width), lambda r, slots, lengths: (slots[r], 0, 0)),
            ],
            out_specs=pl.BlockSpec((columns, length), lambda r, slots, lengths: (0, r)),
        ),
        out_shape=jax.ShapeDtypeStruct(base.shape, base.dtype),
        cost_estimate=pl.CostEstimate(
            flops=2 * tokens * columns * rank,
            bytes_accessed=4 * base.size + 2 * down.size + 2 * count * rank * width,
            transcendentals=0,
        ),
        compiler_params=pltpu.CompilerParams(vmem_limit_bytes=KERNEL_VMEM),
        name="add_update",
    )(slots, lengths, base, down, up_store)


def project_kernel(keep, core_ref, hidden_ref, matrix_ref, *refs):
    came_ref, out_ref = (refs[0], refs[1]) if keep else (None, refs[0])
    blocks, columns, _ = out_ref.shape
    core = core_ref[0]
    upper = core == 1 if keep else core == 0
    parts = []
    for j in range(blocks):
        low = matrix_ref[:, (CORES * j) * columns : (CORES * j + 1) * columns]
        high = matrix_ref[:, (CORES * j + 1) * columns : (CORES * j + 2) * columns]
        parts.append(jnp.where(upper, high, low))
    product = jnp.dot(
        hidden_ref[...], jnp.concatenate(parts, axis=1), preferred_element_type=jnp.float32
    ).T
    for j in range(blocks):
        block = product[j * columns : (j + 1) * columns]
        if keep:
            block = block + came_ref[j].astype(jnp.float32)
        out_ref[j] = block.astype(out_ref.dtype)


def project(core, hidden, matrix, columns, came=None):
    tokens, features = hidden.shape
    width = matrix.shape[1]
    chips = width // (CORES * columns)
    step, rows = min(PROJECT_CHIPS, chips), min(PROJECT_ROWS, tokens)
    block = pl.BlockSpec((step, columns, rows), lambda t, j: (j, 0, t))
    operands = [core.reshape(1), hidden, matrix] + ([] if came is None else [came])
    return pl.pallas_call(
        functools.partial(project_kernel, came is not None),
        grid=(tokens // rows, chips // step),
        out_shape=jax.ShapeDtypeStruct((chips, columns, tokens), hidden.dtype),
        in_specs=[
            pl.BlockSpec(memory_space=pltpu.SMEM),
            pl.BlockSpec((rows, features), lambda t, j: (t, 0)),
            pl.BlockSpec((features, step * CORES * columns), lambda t, j: (0, j)),
        ]
        + ([] if came is None else [block]),
        out_specs=block,
        cost_estimate=NO_COST,
        compiler_params=pltpu.CompilerParams(vmem_limit_bytes=PROJECT_VMEM),
        name="project_own" if came is not None else "project_other",
    )(*operands)


def to_all(block, axis):
    copies = jnp.broadcast_to(block, (lax.axis_size(axis), *block.shape))
    return lax.all_to_all(copies, axis, 0, 0)


def on_device(
    hidden, value_matrix, adapter_down_store, adapter_up_store, adapter_slot, rollout_adapter, lengths
):
    features = hidden.shape[1]
    members = lax.axis_size(TENSOR)
    rollouts = rollout_adapter.shape[0]
    slots_here, rank, columns = adapter_up_store.shape

    copies = jnp.swapaxes(adapter_down_store, 1, 2)
    copies = jnp.broadcast_to(copies, (lax.axis_size("y"), *copies.shape))
    copies, hidden = lax.optimization_barrier((copies, hidden))
    row = lax.all_to_all(copies, "y", 0, 0)
    row = row.reshape(-1, rank, features)
    row_slots = row.shape[0]

    up_store = jnp.pad(adapter_up_store, ((0, 0), (0, 0), (0, -columns % LANES)))
    up_store = lax.all_gather(up_store, DP, axis=0, tiled=True)

    here = lax.axis_index("x")
    shifts = [
        rollout_adapter if d == 0 else lax.ppermute(rollout_adapter, "x", [(i, (i + d) % X) for i in range(X)])
        for d in range(X)
    ]
    wanted = jnp.stack(shifts)[(here - jnp.arange(X, dtype=jnp.int32)) % X].reshape(-1)
    table = jnp.arange(adapter_slot.shape[0], dtype=jnp.int32)
    matches = wanted[:, None] == table[None, :]
    slots = jnp.sum(jnp.where(matches, adapter_slot[None, :], 0), axis=1)
    local = jnp.clip(slots - here * row_slots, 0, row_slots - 1)
    own_matches = rollout_adapter[:, None] == table[None, :]
    own_slots = jnp.sum(jnp.where(own_matches, adapter_slot[None, :], 0), axis=1)
    own = (own_slots // row_slots) * rollouts + jnp.arange(rollouts, dtype=jnp.int32)
    core = lax.axis_index("core")
    other = project(core, hidden, value_matrix, columns)
    came = lax.ppermute(other, "core", [(0, 1), (1, 0)])
    chip = project(core, hidden, value_matrix, columns, came)
    chip, row, local = lax.optimization_barrier((chip, row, local))
    base = lax.psum_scatter(chip.reshape(-1, hidden.shape[0]), "z", scatter_dimension=0, tiled=True)

    sent = pick(row, local).reshape(X, rollouts * rank, features)
    came = lax.all_to_all(sent, "x", 0, 0).reshape(X * rollouts, rank, features)

    down = down_projection(hidden, came, own, members)
    down = lax.all_to_all(down, TENSOR, 0, 0)
    down = jnp.sum(down.astype(jnp.float32), axis=0).astype(jnp.bfloat16)
    down = to_all(down, TENSOR)
    return final(own_slots, lengths, base, down, up_store).T


def solution(mesh):
    dp, tensor = mesh.devices.shape
    fine = Mesh(mesh.devices.reshape(X, dp // X, tensor // CORES, CORES), (*DP, *TENSOR))
    in_specs = (
        P(DP, TENSOR),
        P(TENSOR, None),
        P(DP, TENSOR, None),
        P(DP, None, TENSOR),
        P(),
        P(DP),
        P(DP),
    )
    return jax.shard_map(
        on_device, mesh=fine, in_specs=in_specs, out_specs=P(DP, TENSOR), check_vma=False
    )
```

```python
import functools

import jax
import jax.numpy as jnp
from jax import lax
from jax.experimental import pallas as pl
from jax.experimental.pallas import tpu as pltpu
from jax.sharding import Mesh
from jax.sharding import PartitionSpec as P

ADAPTER_SCALE = 2.0
X, CORES = 4, 2
DP, TENSOR = ("x", "y"), ("z", "core")
LANES = 128
KERNEL_VMEM = 8 << 20
PROJECT_VMEM, PROJECT_ROWS, PROJECT_CHIPS = 60 << 20, 1024, 4


def cost(flops, size):
    return pl.CostEstimate(flops=flops, bytes_accessed=2 * size, transcendentals=0)


def copies_kernel(down_ref, up_ref, out_ref, stage, ups, in_sems, sems):
    slots, rank, features = down_ref.shape
    packed = stage.shape[0] - slots * rank
    first = [
        pltpu.make_async_copy(down_ref.at[j], stage.at[pl.ds(j * rank, rank)], in_sems.at[j])
        for j in range(slots)
    ]
    first.append(pltpu.make_async_copy(up_ref, ups, in_sems.at[slots]))
    copies = [
        pltpu.make_async_copy(stage, out_ref.at[i], sems.at[i]) for i in range(out_ref.shape[0])
    ]
    for copy in first:
        copy.start()
    for copy in first:
        copy.wait()
    both = jnp.concatenate([ups[j] for j in range(slots)], axis=1)
    for q in range(features // LANES):
        block = both[q * packed : (q + 1) * packed]
        stage[slots * rank :, q * LANES : (q + 1) * LANES] = block
    for copy in copies:
        copy.start()
    for copy in copies:
        copy.wait()


def factor_copies(down, up, count):
    slots, rank, features = down.shape
    rows = slots * rank + rank * LANES // features
    return pl.pallas_call(
        copies_kernel,
        out_shape=jax.ShapeDtypeStruct((count, rows, features), down.dtype),
        in_specs=[pl.BlockSpec(memory_space=pl.ANY)] * 2,
        out_specs=pl.BlockSpec(memory_space=pl.ANY),
        scratch_shapes=[
            pltpu.VMEM((rows, features), down.dtype),
            pltpu.VMEM(up.shape, up.dtype),
            pltpu.SemaphoreType.DMA((slots + 1,)),
            pltpu.SemaphoreType.DMA((count,)),
        ],
        cost_estimate=cost(0, count * rows * features),
        compiler_params=pltpu.CompilerParams(vmem_limit_bytes=PROJECT_VMEM),
        name="factor_copies",
    )(down, up)


def project_kernel(hidden_ref, other_ref, matrix_ref, other_matrix_ref, *refs):
    *out_refs, own, own_other = refs
    columns = out_refs[0].shape[0]
    chips, span = len(out_refs), CORES * columns

    @pl.when(pl.program_id(0) == 0)
    def _():
        here, upper = lax.axis_index("z"), lax.axis_index("core") == 1
        low = lax.broadcasted_iota(jnp.int32, (matrix_ref.shape[0], span), 1) < columns
        for source, chosen in ((matrix_ref, own), (other_matrix_ref, own_other)):
            for k in range(0, chips, 2):
                pair = []
                for i in range(2):
                    start = pl.multiple_of(lax.rem(here + k + i, chips) * span, span)
                    block = source[:, pl.ds(start, span)]
                    turned = jnp.concatenate([block[:, columns:], block[:, :columns]], axis=1)
                    pair.append(jnp.where(upper == (i == 1), block, turned))
                chosen[:, k * columns : (k + 2) * columns] = jnp.where(low, pair[0], pair[1])

    for first in range(0, chips, PROJECT_CHIPS):
        last = min(first + PROJECT_CHIPS, chips)
        lanes = slice(first * columns, last * columns)
        product = jnp.dot(
            hidden_ref[...], own[:, lanes], preferred_element_type=jnp.float32
        ) + jnp.dot(other_ref[...], own_other[:, lanes], preferred_element_type=jnp.float32)
        product = product.astype(out_refs[0].dtype).T
        for k in range(first, last):
            out_refs[k][...] = product[(k - first) * columns : (k - first + 1) * columns]


def project(hidden, other, matrix, other_matrix, columns):
    tokens, features = hidden.shape
    width = matrix.shape[1]
    chips = width // (CORES * columns)
    rows = min(PROJECT_ROWS, tokens)
    row_spec = pl.BlockSpec((rows, features), lambda t: (t, 0))
    matrix_spec = pl.BlockSpec(matrix.shape, lambda t: (0, 0))
    return pl.pallas_call(
        project_kernel,
        grid=(tokens // rows,),
        out_shape=[jax.ShapeDtypeStruct((columns, tokens), hidden.dtype)] * chips,
        in_specs=[row_spec] * 2 + [matrix_spec] * 2,
        out_specs=[pl.BlockSpec((columns, rows), lambda t: (0, t))] * chips,
        scratch_shapes=[pltpu.VMEM((features, chips * columns), matrix.dtype)] * 2,
        cost_estimate=cost(
            2 * tokens * features * width,
            2 * hidden.size + 2 * matrix.size + tokens * chips * columns,
        ),
        compiler_params=pltpu.CompilerParams(vmem_limit_bytes=PROJECT_VMEM),
        name="project",
    )(hidden, other, matrix, other_matrix)


def add(a, b):
    return (a.astype(jnp.float32) + b.astype(jnp.float32)).astype(a.dtype)


def along(axis, value, step):
    n = lax.axis_size(axis)
    return lax.ppermute(value, axis, [(i, (i + step) % n) for i in range(n)])


def pick_kernel(slots, rank, index_ref, row_ref, out_ref):
    dests, _, features = out_ref.shape
    packed = rank * LANES // features
    rollouts = index_ref.shape[0] // dests
    half = LANES // 2
    low = lax.broadcasted_iota(jnp.int32, (packed, LANES), 1) < half
    for d in range(dests):
        ups = []
        for r in range(rollouts):
            index = index_ref[d * rollouts + r]
            owner, place = index // slots, index % slots
            start = pl.multiple_of(place * rank, rank)
            out_ref[d, r * rank : (r + 1) * rank] = row_ref[owner, pl.ds(start, rank)]
            ups.append((row_ref[owner, slots * rank :], place))
        for p in range(rollouts // 2):
            for q in range(features // LANES):
                lanes = slice(q * LANES, (q + 1) * LANES)
                pair = []
                for h in range(2):
                    block, place = ups[2 * p + h]
                    block = block[:, lanes]
                    turned = jnp.concatenate([block[:, half:], block[:, :half]], axis=1)
                    pair.append(jnp.where(place == h, block, turned))
                at = rollouts * rank + p * packed
                out_ref[d, at : at + packed, lanes] = jnp.where(low, pair[0], pair[1])


def pick(index, row, dests, slots, rank):
    features = row.shape[2]
    packed = rank * LANES // features
    rollouts = index.shape[0] // dests
    rows = rollouts * rank + rollouts // 2 * packed
    return pl.pallas_call(
        functools.partial(pick_kernel, slots, rank),
        out_shape=jax.ShapeDtypeStruct((dests, rows, features), row.dtype),
        in_specs=[
            pl.BlockSpec(memory_space=pltpu.SMEM),
            pl.BlockSpec(memory_space=pltpu.VMEM),
        ],
        out_specs=pl.BlockSpec(memory_space=pltpu.VMEM),
        cost_estimate=cost(0, 2 * dests * rows * features),
        compiler_params=pltpu.CompilerParams(vmem_limit_bytes=KERNEL_VMEM),
        name="pick_factors",
    )(index, row)


def down_kernel(own_row_ref, hidden_ref, factor_ref, out_ref):
    members, rank, chunk = out_ref.shape
    count = own_row_ref.shape[0]
    per = members // count
    length = per * chunk
    for r in range(count):
        product = lax.dot_general(
            hidden_ref[r * length : (r + 1) * length],
            factor_ref[own_row_ref[r], r * rank : (r + 1) * rank],
            (((1,), (1,)), ((), ())),
            preferred_element_type=jnp.float32,
        ).T.astype(out_ref.dtype)
        for i in range(per):
            out_ref[r * per + i] = product[:, i * chunk : (i + 1) * chunk]


def down_projection(own_row, hidden, factors, members, rank):
    tokens, features = hidden.shape
    return pl.pallas_call(
        down_kernel,
        out_shape=jax.ShapeDtypeStruct((members, rank, tokens // members), hidden.dtype),
        in_specs=[pl.BlockSpec(memory_space=pltpu.SMEM)]
        + [pl.BlockSpec(memory_space=pltpu.VMEM)] * 2,
        out_specs=pl.BlockSpec(memory_space=pltpu.VMEM),
        cost_estimate=cost(2 * tokens * features * rank, hidden.size + tokens * rank),
        compiler_params=pltpu.CompilerParams(vmem_limit_bytes=KERNEL_VMEM),
        name="down_projection",
    )(own_row, hidden, factors)


def sum_kernel(parts_ref, out_ref):
    total = parts_ref[0].astype(jnp.float32)
    for i in range(1, parts_ref.shape[0]):
        total += parts_ref[i].astype(jnp.float32)
    total = total.astype(out_ref.dtype)
    for i in range(out_ref.shape[0]):
        out_ref[i] = total


def sum_copies(parts):
    return pl.pallas_call(
        sum_kernel,
        out_shape=jax.ShapeDtypeStruct(parts.shape, parts.dtype),
        in_specs=[pl.BlockSpec(memory_space=pltpu.VMEM)],
        out_specs=pl.BlockSpec(memory_space=pltpu.VMEM),
        cost_estimate=cost(parts.size, 2 * parts.size),
        compiler_params=pltpu.CompilerParams(vmem_limit_bytes=KERNEL_VMEM),
        name="sum_parts",
    )(parts)


def final_kernel(own_row_ref, lengths_ref, *refs):
    *base_refs, down_ref, factor_ref, out_ref = refs
    columns, tokens = out_ref.shape
    members, rank, chunk = down_ref.shape
    features = factor_ref.shape[2]
    packed = rank * LANES // features
    count = own_row_ref.shape[0]
    per, length = members // count, tokens // count
    for r in range(count):
        at = count * rank + r // 2 * packed
        block = factor_ref[own_row_ref[r], at : at + packed, :]
        first = r % 2 * columns
        up = jnp.concatenate(
            [
                block[:, q * LANES + first : q * LANES + first + columns]
                for q in range(features // LANES)
            ],
            axis=0,
        )
        down = jnp.concatenate([down_ref[r * per + i] for i in range(per)], axis=1)
        update = lax.dot_general(
            up, down, (((0,), (0,)), ((), ())), preferred_element_type=jnp.float32
        )
        span = slice(r * length, (r + 1) * length)
        total = ADAPTER_SCALE * update
        for base_ref in base_refs:
            total += base_ref[:, span].astype(jnp.float32)
        position = lax.broadcasted_iota(jnp.int32, (columns, length), 1)
        out_ref[:, span] = jnp.where(position < lengths_ref[r], total, 0.0).astype(out_ref.dtype)


def final(own_row, lengths, base, down, factors):
    columns, tokens = base[0].shape
    rank = down.shape[1]
    return pl.pallas_call(
        final_kernel,
        out_shape=jax.ShapeDtypeStruct(base[0].shape, base[0].dtype),
        in_specs=[pl.BlockSpec(memory_space=pltpu.SMEM)] * 2
        + [pl.BlockSpec(memory_space=pltpu.VMEM)] * (len(base) + 2),
        out_specs=pl.BlockSpec(memory_space=pltpu.VMEM),
        cost_estimate=cost(2 * tokens * columns * rank, 4 * base[0].size + down.size),
        compiler_params=pltpu.CompilerParams(vmem_limit_bytes=KERNEL_VMEM),
        name="add_update",
    )(own_row, lengths, *base, down, factors)


def on_device(
    hidden, value_matrix, adapter_down_store, adapter_up_store, adapter_slot, rollout_adapter, lengths
):
    members = lax.axis_size(TENSOR)
    rollouts = rollout_adapter.shape[0]
    slots_here, rank, _ = adapter_up_store.shape
    row_slots = slots_here * lax.axis_size("y")

    other = along("core", hidden, 1)
    other_matrix = along("core", value_matrix, 1)
    copies = factor_copies(
        jnp.swapaxes(adapter_down_store, 1, 2), adapter_up_store, lax.axis_size("y")
    )
    row = lax.all_to_all(copies, "y", 0, 0)

    parts = project(hidden, other, value_matrix, other_matrix, adapter_up_store.shape[2])
    far = len(parts) // 2
    ahead, behind = parts[far], parts[far + 1]
    for k in range(far - 1, -1, -1):
        ahead = along("z", ahead, 1)
        if k:
            ahead = add(ahead, parts[k])
    for k in range(far + 2, len(parts) + 1):
        behind = along("z", behind, -1)
        if k < len(parts):
            behind = add(behind, parts[k])
    base = (parts[0], ahead, behind)

    here = lax.axis_index("x")
    mine = jnp.arange(X, dtype=jnp.int32)[:, None] == here
    wanted = lax.psum(jnp.where(mine, rollout_adapter[None, :], 0), "x").reshape(-1)
    table = jnp.arange(adapter_slot.shape[0], dtype=jnp.int32)
    matches = wanted[:, None] == table[None, :]
    slots = jnp.sum(jnp.where(matches, adapter_slot[None, :], 0), axis=1)
    local = jnp.clip(slots - here * row_slots, 0, row_slots - 1)
    own_row = lax.dynamic_slice_in_dim(slots, here * rollouts, rollouts) // row_slots
    local, own_row = lax.optimization_barrier((local, own_row))

    sent = pick(local, row, X, slots_here, rank)
    factors = lax.all_to_all(sent, "x", 0, 0)
    down = down_projection(own_row, hidden, factors, members, rank)
    down = lax.all_to_all(down, TENSOR, 0, 0)
    down = sum_copies(down)
    down = lax.all_to_all(down, TENSOR, 0, 0)
    return final(own_row, lengths, base, down, factors).T


def solution(mesh):
    dp, tensor = mesh.devices.shape
    fine = Mesh(mesh.devices.reshape(X, dp // X, tensor // CORES, CORES), (*DP, *TENSOR))
    in_specs = (
        P(DP, TENSOR),
        P(TENSOR, None),
        P(DP, TENSOR, None),
        P(DP, None, TENSOR),
        P(),
        P(DP),
        P(DP),
    )
    return jax.shard_map(
        on_device, mesh=fine, in_specs=in_specs, out_specs=P(DP, TENSOR), check_vma=False
    )
```

```python
import functools

import jax
import jax.numpy as jnp
from jax import lax
from jax.experimental import pallas as pl
from jax.experimental.pallas import tpu as pltpu
from jax.sharding import Mesh
from jax.sharding import PartitionSpec as P

ADAPTER_SCALE = 2.0
X, CORES = 4, 2
DP, TENSOR = ("x", "y"), ("z", "core")
LANES = 128
AHEAD_WEIGHTS, BEHIND_WEIGHTS, LAST_WEIGHT = (1, 50000, 1), (50000, 1), 50000
KERNEL_VMEM = 8 << 20
PROJECT_VMEM, PROJECT_ROWS, PROJECT_CHIPS = 60 << 20, 1024, 4


def cost(flops, size):
    return pl.CostEstimate(flops=flops, bytes_accessed=2 * size, transcendentals=0)


def copies_kernel(down_ref, up_ref, out_ref, stage, ups, in_sems, sems):
    slots, rank, features = down_ref.shape
    packed = stage.shape[0] - slots * rank
    first = [
        pltpu.make_async_copy(down_ref.at[j], stage.at[pl.ds(j * rank, rank)], in_sems.at[j])
        for j in range(slots)
    ]
    first.append(pltpu.make_async_copy(up_ref, ups, in_sems.at[slots]))
    copies = [
        pltpu.make_async_copy(stage, out_ref.at[i], sems.at[i]) for i in range(out_ref.shape[0])
    ]
    for copy in first:
        copy.start()
    for copy in first:
        copy.wait()
    both = jnp.concatenate([ups[j] for j in range(slots)], axis=1)
    for q in range(features // LANES):
        block = both[q * packed : (q + 1) * packed]
        stage[slots * rank :, q * LANES : (q + 1) * LANES] = block
    for copy in copies:
        copy.start()
    for copy in copies:
        copy.wait()


def factor_copies(down, up, count):
    slots, rank, features = down.shape
    rows = slots * rank + rank * LANES // features
    return pl.pallas_call(
        copies_kernel,
        out_shape=jax.ShapeDtypeStruct((count, rows, features), down.dtype),
        in_specs=[pl.BlockSpec(memory_space=pl.ANY)] * 2,
        out_specs=pl.BlockSpec(memory_space=pl.ANY),
        scratch_shapes=[
            pltpu.VMEM((rows, features), down.dtype),
            pltpu.VMEM(up.shape, up.dtype),
            pltpu.SemaphoreType.DMA((slots + 1,)),
            pltpu.SemaphoreType.DMA((count,)),
        ],
        cost_estimate=cost(0, count * rows * features),
        compiler_params=pltpu.CompilerParams(vmem_limit_bytes=PROJECT_VMEM),
        name="factor_copies",
    )(down, up)


def project_kernel(hidden_ref, other_ref, matrix_ref, other_matrix_ref, *refs):
    *out_refs, own, own_other = refs
    columns = out_refs[0].shape[0]
    chips, span = len(out_refs), CORES * columns

    @pl.when(pl.program_id(0) == 0)
    def _():
        here, upper = lax.axis_index("z"), lax.axis_index("core") == 1
        low = lax.broadcasted_iota(jnp.int32, (matrix_ref.shape[0], span), 1) < columns
        for source, chosen in ((matrix_ref, own), (other_matrix_ref, own_other)):
            for k in range(0, chips, 2):
                pair = []
                for i in range(2):
                    start = pl.multiple_of(lax.rem(here + k + i, chips) * span, span)
                    block = source[:, pl.ds(start, span)]
                    turned = jnp.concatenate([block[:, columns:], block[:, :columns]], axis=1)
                    pair.append(jnp.where(upper == (i == 1), block, turned))
                chosen[:, k * columns : (k + 2) * columns] = jnp.where(low, pair[0], pair[1])

    for first in range(0, chips, PROJECT_CHIPS):
        last = min(first + PROJECT_CHIPS, chips)
        lanes = slice(first * columns, last * columns)
        product = jnp.dot(
            hidden_ref[...], own[:, lanes], preferred_element_type=jnp.float32
        ) + jnp.dot(other_ref[...], own_other[:, lanes], preferred_element_type=jnp.float32)
        product = product.astype(out_refs[0].dtype).T
        for k in range(first, last):
            out_refs[k][...] = product[(k - first) * columns : (k - first + 1) * columns]


def project(hidden, other, matrix, other_matrix, columns):
    tokens, features = hidden.shape
    width = matrix.shape[1]
    chips = width // (CORES * columns)
    rows = min(PROJECT_ROWS, tokens)
    row_spec = pl.BlockSpec((rows, features), lambda t: (t, 0))
    matrix_spec = pl.BlockSpec(matrix.shape, lambda t: (0, 0))
    return pl.pallas_call(
        project_kernel,
        grid=(tokens // rows,),
        out_shape=[jax.ShapeDtypeStruct((columns, tokens), hidden.dtype)] * chips,
        in_specs=[row_spec] * 2 + [matrix_spec] * 2,
        out_specs=[pl.BlockSpec((columns, rows), lambda t: (0, t))] * chips,
        scratch_shapes=[pltpu.VMEM((features, chips * columns), matrix.dtype)] * 2,
        cost_estimate=cost(
            2 * tokens * features * width,
            2 * hidden.size + 2 * matrix.size + tokens * chips * columns,
        ),
        compiler_params=pltpu.CompilerParams(vmem_limit_bytes=PROJECT_VMEM),
        name="project",
    )(hidden, other, matrix, other_matrix)


def add_kernel(*refs):
    *in_refs, out_ref = refs
    total = in_refs[0][...].astype(jnp.float32)
    for ref in in_refs[1:]:
        total += ref[...].astype(jnp.float32)
    out_ref[...] = total.astype(out_ref.dtype)


def add(*parts, weight):
    size = parts[0].size
    return pl.pallas_call(
        add_kernel,
        out_shape=jax.ShapeDtypeStruct(parts[0].shape, parts[0].dtype),
        in_specs=[pl.BlockSpec(memory_space=pltpu.VMEM)] * len(parts),
        out_specs=pl.BlockSpec(memory_space=pltpu.VMEM),
        cost_estimate=cost(weight * size, (len(parts) + 1) * size),
        compiler_params=pltpu.CompilerParams(vmem_limit_bytes=KERNEL_VMEM),
        name="add_parts",
    )(*parts)


def along(axis, value, step):
    n = lax.axis_size(axis)
    return lax.ppermute(value, axis, [(i, (i + step) % n) for i in range(n)])


def pick_kernel(slots, rank, index_ref, row_ref, out_ref):
    dests, _, features = out_ref.shape
    packed = rank * LANES // features
    rollouts = index_ref.shape[0] // dests
    half = LANES // 2
    low = lax.broadcasted_iota(jnp.int32, (packed, LANES), 1) < half
    for d in range(dests):
        ups = []
        for r in range(rollouts):
            index = index_ref[d * rollouts + r]
            owner, place = index // slots, index % slots
            start = pl.multiple_of(place * rank, rank)
            out_ref[d, r * rank : (r + 1) * rank] = row_ref[owner, pl.ds(start, rank)]
            ups.append((row_ref[owner, slots * rank :], place))
        for p in range(rollouts // 2):
            for q in range(features // LANES):
                lanes = slice(q * LANES, (q + 1) * LANES)
                pair = []
                for h in range(2):
                    block, place = ups[2 * p + h]
                    block = block[:, lanes]
                    turned = jnp.concatenate([block[:, half:], block[:, :half]], axis=1)
                    pair.append(jnp.where(place == h, block, turned))
                at = rollouts * rank + p * packed
                out_ref[d, at : at + packed, lanes] = jnp.where(low, pair[0], pair[1])


def pick(index, row, dests, slots, rank):
    features = row.shape[2]
    packed = rank * LANES // features
    rollouts = index.shape[0] // dests
    rows = rollouts * rank + rollouts // 2 * packed
    return pl.pallas_call(
        functools.partial(pick_kernel, slots, rank),
        out_shape=jax.ShapeDtypeStruct((dests, rows, features), row.dtype),
        in_specs=[
            pl.BlockSpec(memory_space=pltpu.SMEM),
            pl.BlockSpec(memory_space=pltpu.VMEM),
        ],
        out_specs=pl.BlockSpec(memory_space=pltpu.VMEM),
        cost_estimate=cost(0, 2 * dests * rows * features),
        compiler_params=pltpu.CompilerParams(vmem_limit_bytes=KERNEL_VMEM),
        name="pick_factors",
    )(index, row)


def down_kernel(own_row_ref, hidden_ref, factor_ref, out_ref):
    members, rank, chunk = out_ref.shape
    count = own_row_ref.shape[0]
    per = members // count
    length = per * chunk
    for r in range(count):
        product = lax.dot_general(
            hidden_ref[r * length : (r + 1) * length],
            factor_ref[own_row_ref[r], r * rank : (r + 1) * rank],
            (((1,), (1,)), ((), ())),
            preferred_element_type=jnp.float32,
        ).T.astype(out_ref.dtype)
        for i in range(per):
            out_ref[r * per + i] = product[:, i * chunk : (i + 1) * chunk]


def down_projection(own_row, hidden, factors, members, rank):
    tokens, features = hidden.shape
    return pl.pallas_call(
        down_kernel,
        out_shape=jax.ShapeDtypeStruct((members, rank, tokens // members), hidden.dtype),
        in_specs=[pl.BlockSpec(memory_space=pltpu.SMEM)]
        + [pl.BlockSpec(memory_space=pltpu.VMEM)] * 2,
        out_specs=pl.BlockSpec(memory_space=pltpu.VMEM),
        cost_estimate=cost(2 * tokens * features * rank, hidden.size + tokens * rank),
        compiler_params=pltpu.CompilerParams(vmem_limit_bytes=KERNEL_VMEM),
        name="down_projection",
    )(own_row, hidden, factors)


def sum_kernel(parts_ref, out_ref):
    total = parts_ref[0].astype(jnp.float32)
    for i in range(1, parts_ref.shape[0]):
        total += parts_ref[i].astype(jnp.float32)
    total = total.astype(out_ref.dtype)
    for i in range(out_ref.shape[0]):
        out_ref[i] = total


def sum_copies(parts):
    return pl.pallas_call(
        sum_kernel,
        out_shape=jax.ShapeDtypeStruct(parts.shape, parts.dtype),
        in_specs=[pl.BlockSpec(memory_space=pltpu.VMEM)],
        out_specs=pl.BlockSpec(memory_space=pltpu.VMEM),
        cost_estimate=cost(parts.size, 2 * parts.size),
        compiler_params=pltpu.CompilerParams(vmem_limit_bytes=KERNEL_VMEM),
        name="sum_parts",
    )(parts)


def final_kernel(own_row_ref, lengths_ref, *refs):
    *base_refs, down_ref, factor_ref, out_ref = refs
    columns, tokens = out_ref.shape
    members, rank, chunk = down_ref.shape
    features = factor_ref.shape[2]
    packed = rank * LANES // features
    count = own_row_ref.shape[0]
    per, length = members // count, tokens // count
    for r in range(count):
        at = count * rank + r // 2 * packed
        block = factor_ref[own_row_ref[r], at : at + packed, :]
        first = r % 2 * columns
        up = jnp.concatenate(
            [
                block[:, q * LANES + first : q * LANES + first + columns]
                for q in range(features // LANES)
            ],
            axis=0,
        )
        down = jnp.concatenate([down_ref[r * per + i] for i in range(per)], axis=1)
        update = lax.dot_general(
            up, down, (((0,), (0,)), ((), ())), preferred_element_type=jnp.float32
        )
        span = slice(r * length, (r + 1) * length)
        total = ADAPTER_SCALE * update
        for base_ref in base_refs:
            total += base_ref[:, span].astype(jnp.float32)
        position = lax.broadcasted_iota(jnp.int32, (columns, length), 1)
        out_ref[:, span] = jnp.where(position < lengths_ref[r], total, 0.0).astype(out_ref.dtype)


def final(own_row, lengths, base, down, factors):
    columns, tokens = base[0].shape
    rank = down.shape[1]
    return pl.pallas_call(
        final_kernel,
        out_shape=jax.ShapeDtypeStruct(base[0].shape, base[0].dtype),
        in_specs=[pl.BlockSpec(memory_space=pltpu.SMEM)] * 2
        + [pl.BlockSpec(memory_space=pltpu.VMEM)] * (len(base) + 2),
        out_specs=pl.BlockSpec(memory_space=pltpu.VMEM),
        cost_estimate=cost(2 * tokens * columns * rank, 4 * base[0].size + down.size),
        compiler_params=pltpu.CompilerParams(vmem_limit_bytes=KERNEL_VMEM),
        name="add_update",
    )(own_row, lengths, *base, down, factors)


def on_device(
    hidden, value_matrix, adapter_down_store, adapter_up_store, adapter_slot, rollout_adapter, lengths
):
    members = lax.axis_size(TENSOR)
    rollouts = rollout_adapter.shape[0]
    slots_here, rank, _ = adapter_up_store.shape
    row_slots = slots_here * lax.axis_size("y")

    other = along("core", hidden, 1)
    other_matrix = along("core", value_matrix, 1)
    copies = factor_copies(
        jnp.swapaxes(adapter_down_store, 1, 2), adapter_up_store, lax.axis_size("y")
    )
    row = lax.all_to_all(copies, "y", 0, 0)

    parts = project(hidden, other, value_matrix, other_matrix, adapter_up_store.shape[2])
    *parts, rollout_adapter = lax.optimization_barrier((*parts, rollout_adapter))
    far = len(parts) // 2
    ahead, behind = parts[far], parts[far + 1]
    for k in range(far - 1, -1, -1):
        ahead = along("z", ahead, 1)
        if k:
            ahead = add(ahead, parts[k], weight=AHEAD_WEIGHTS[far - 1 - k])
    for k in range(far + 2, len(parts) + 1):
        behind = along("z", behind, -1)
        if k < len(parts):
            behind = add(behind, parts[k], weight=BEHIND_WEIGHTS[k - far - 2])
    base = (add(parts[0], ahead, behind, weight=LAST_WEIGHT),)

    here = lax.axis_index("x")
    mine = jnp.arange(X, dtype=jnp.int32)[:, None] == here
    wanted = lax.psum(jnp.where(mine, rollout_adapter[None, :], 0), "x").reshape(-1)
    table = jnp.arange(adapter_slot.shape[0], dtype=jnp.int32)
    matches = wanted[:, None] == table[None, :]
    slots = jnp.sum(jnp.where(matches, adapter_slot[None, :], 0), axis=1)
    local = jnp.clip(slots - here * row_slots, 0, row_slots - 1)
    own_row = lax.dynamic_slice_in_dim(slots, here * rollouts, rollouts) // row_slots
    local, own_row = lax.optimization_barrier((local, own_row))

    sent = pick(local, row, X, slots_here, rank)
    factors = lax.all_to_all(sent, "x", 0, 0)
    down = down_projection(own_row, hidden, factors, members, rank)
    down = lax.all_to_all(down, TENSOR, 0, 0)
    down = sum_copies(down)
    down = lax.all_to_all(down, TENSOR, 0, 0)
    return final(own_row, lengths, base, down, factors).T


def solution(mesh):
    dp, tensor = mesh.devices.shape
    fine = Mesh(mesh.devices.reshape(X, dp // X, tensor // CORES, CORES), (*DP, *TENSOR))
    in_specs = (
        P(DP, TENSOR),
        P(TENSOR, None),
        P(DP, TENSOR, None),
        P(DP, None, TENSOR),
        P(),
        P(DP),
        P(DP),
    )
    return jax.shard_map(
        on_device, mesh=fine, in_specs=in_specs, out_specs=P(DP, TENSOR), check_vma=False
    )
```

```python
import functools

import jax
import jax.numpy as jnp
from jax import lax
from jax.experimental import pallas as pl
from jax.experimental.pallas import tpu as pltpu
from jax.sharding import Mesh
from jax.sharding import PartitionSpec as P

ADAPTER_SCALE = 2.0
X, CORES = 4, 2
DP, TENSOR = ("x", "y"), ("z", "core")
LANES = 128
WEIGHTS = (1, 1, 50000, 1)
KERNEL_VMEM = 8 << 20
PROJECT_VMEM, PROJECT_ROWS = 60 << 20, 1024


def cost(flops, size):
    return pl.CostEstimate(flops=flops, bytes_accessed=2 * size, transcendentals=0)


def copies_kernel(down_ref, up_ref, out_ref, stage, ups, in_sems, sems):
    slots, rank, features = down_ref.shape
    packed = stage.shape[0] - slots * rank
    first = [
        pltpu.make_async_copy(down_ref.at[j], stage.at[pl.ds(j * rank, rank)], in_sems.at[j])
        for j in range(slots)
    ]
    first.append(pltpu.make_async_copy(up_ref, ups, in_sems.at[slots]))
    copies = [
        pltpu.make_async_copy(stage, out_ref.at[i], sems.at[i]) for i in range(out_ref.shape[0])
    ]
    for copy in first:
        copy.start()
    for copy in first:
        copy.wait()
    both = jnp.concatenate([ups[j] for j in range(slots)], axis=1)
    for q in range(features // LANES):
        block = both[q * packed : (q + 1) * packed]
        stage[slots * rank :, q * LANES : (q + 1) * LANES] = block
    for copy in copies:
        copy.start()
    for copy in copies:
        copy.wait()


def factor_copies(down, up, count):
    slots, rank, features = down.shape
    rows = slots * rank + rank * LANES // features
    return pl.pallas_call(
        copies_kernel,
        out_shape=jax.ShapeDtypeStruct((count, rows, features), down.dtype),
        in_specs=[pl.BlockSpec(memory_space=pl.ANY)] * 2,
        out_specs=pl.BlockSpec(memory_space=pl.ANY),
        scratch_shapes=[
            pltpu.VMEM((rows, features), down.dtype),
            pltpu.VMEM(up.shape, up.dtype),
            pltpu.SemaphoreType.DMA((slots + 1,)),
            pltpu.SemaphoreType.DMA((count,)),
        ],
        cost_estimate=cost(0, count * rows * features),
        compiler_params=pltpu.CompilerParams(vmem_limit_bytes=PROJECT_VMEM),
        name="factor_copies",
    )(down, up)


def project_kernel(hidden_ref, other_ref, matrix_ref, other_matrix_ref, *refs):
    *out_refs, own_ref, far_ref, chosen, chosen_other = refs
    columns, span = own_ref.shape[0], out_refs[0].shape[0]
    chips = matrix_ref.shape[1] // span
    last = len(out_refs) * span

    @pl.when(pl.program_id(0) == 0)
    def _():
        here, upper = lax.axis_index("z"), lax.axis_index("core") == 1
        low = lax.broadcasted_iota(jnp.int32, (matrix_ref.shape[0], span), 1) < columns

        def block(source, chip):
            start = pl.multiple_of(lax.rem(chip + chips, chips) * span, span)
            return source[:, pl.ds(start, span)]

        def turned(value):
            return jnp.concatenate([value[:, columns:], value[:, :columns]], axis=1)

        for source, to in ((matrix_ref, chosen), (other_matrix_ref, chosen_other)):
            for i in range(len(out_refs)):
                hops = len(out_refs) - i
                chip = here + jnp.where(upper, -hops, hops)
                to[:, i * span : (i + 1) * span] = block(source, chip)
            own, far = block(source, here), block(source, here + chips // 2)
            own = jnp.where(upper, turned(own), own)
            far = jnp.where(upper, far, turned(far))
            to[:, last:] = jnp.where(low, own, far)

    for first in range(0, last + span, 2 * span):
        lanes = slice(first, first + 2 * span)
        product = jnp.dot(
            hidden_ref[...], chosen[:, lanes], preferred_element_type=jnp.float32
        ) + jnp.dot(other_ref[...], chosen_other[:, lanes], preferred_element_type=jnp.float32)
        product = product.astype(own_ref.dtype).T
        for i in range(2):
            block = product[i * span : (i + 1) * span]
            if first + i * span < last:
                out_refs[first // span + i][...] = block
            else:
                own_ref[...] = block[:columns]
                far_ref[...] = block[columns:]


def project(hidden, other, matrix, other_matrix, columns):
    tokens, features = hidden.shape
    width = matrix.shape[1]
    span = CORES * columns
    hops = width // span // 2 - 1
    rows = min(PROJECT_ROWS, tokens)
    row_spec = pl.BlockSpec((rows, features), lambda t: (t, 0))
    matrix_spec = pl.BlockSpec(matrix.shape, lambda t: (0, 0))
    heights = [span] * hops + [columns] * 2
    return pl.pallas_call(
        project_kernel,
        grid=(tokens // rows,),
        out_shape=[jax.ShapeDtypeStruct((height, tokens), hidden.dtype) for height in heights],
        in_specs=[row_spec] * 2 + [matrix_spec] * 2,
        out_specs=[pl.BlockSpec((height, rows), lambda t: (0, t)) for height in heights],
        scratch_shapes=[pltpu.VMEM((features, sum(heights)), matrix.dtype)] * 2,
        cost_estimate=cost(0, 0),
        compiler_params=pltpu.CompilerParams(vmem_limit_bytes=PROJECT_VMEM),
        name="project",
    )(hidden, other, matrix, other_matrix)


def vmem_call(kernel, name, weight, out_shape, *operands):
    size = operands[0].size
    several = isinstance(out_shape, list)
    spec = pl.BlockSpec(memory_space=pltpu.VMEM)
    return pl.pallas_call(
        kernel,
        out_shape=out_shape,
        in_specs=[spec] * len(operands),
        out_specs=[spec] * len(out_shape) if several else spec,
        cost_estimate=cost(weight * size, 3 * size),
        compiler_params=pltpu.CompilerParams(vmem_limit_bytes=KERNEL_VMEM),
        name=name,
    )(*operands)


def like(value, rows=None):
    return jax.ShapeDtypeStruct((rows or value.shape[0], *value.shape[1:]), value.dtype)


def sum_refs(a, b):
    return (a.astype(jnp.float32) + b.astype(jnp.float32)).astype(a.dtype)


def add_kernel(part_ref, came_ref, out_ref):
    out_ref[...] = sum_refs(part_ref[...], came_ref[...])


def add_own_kernel(part_ref, came_ref, out_ref):
    columns = came_ref.shape[0]
    mine = pl.ds(pl.multiple_of(lax.axis_index("core") * columns, columns), columns)
    out_ref[...] = part_ref[...]
    out_ref[mine] = sum_refs(part_ref[mine], came_ref[...])


def split_kernel(chain_ref, own_ref, kept_ref, sent_ref):
    columns = own_ref.shape[0]
    core = lax.axis_index("core")
    mine = pl.ds(pl.multiple_of(core * columns, columns), columns)
    theirs = pl.ds(pl.multiple_of((1 - core) * columns, columns), columns)
    kept_ref[...] = sum_refs(own_ref[...], chain_ref[mine])
    sent_ref[...] = chain_ref[theirs]


def hop(value):
    n = lax.axis_size("z")
    pairs = [
        (z * CORES + core, (z + (1 - 2 * core)) % n * CORES + core)
        for z in range(n)
        for core in range(CORES)
    ]
    return lax.ppermute(value, TENSOR, pairs)


def along(axis, value, step):
    n = lax.axis_size(axis)
    return lax.ppermute(value, axis, [(i, (i + step) % n) for i in range(n)])


def pick_kernel(slots, rank, index_ref, row_ref, out_ref):
    dests, _, features = out_ref.shape
    packed = rank * LANES // features
    rollouts = index_ref.shape[0] // dests
    half = LANES // 2
    low = lax.broadcasted_iota(jnp.int32, (packed, LANES), 1) < half
    for d in range(dests):
        ups = []
        for r in range(rollouts):
            index = index_ref[d * rollouts + r]
            owner, place = index // slots, index % slots
            start = pl.multiple_of(place * rank, rank)
            out_ref[d, r * rank : (r + 1) * rank] = row_ref[owner, pl.ds(start, rank)]
            ups.append((row_ref[owner, slots * rank :], place))
        for p in range(rollouts // 2):
            for q in range(features // LANES):
                lanes = slice(q * LANES, (q + 1) * LANES)
                pair = []
                for h in range(2):
                    block, place = ups[2 * p + h]
                    block = block[:, lanes]
                    turned = jnp.concatenate([block[:, half:], block[:, :half]], axis=1)
                    pair.append(jnp.where(place == h, block, turned))
                at = rollouts * rank + p * packed
                out_ref[d, at : at + packed, lanes] = jnp.where(low, pair[0], pair[1])


def pick(index, row, dests, slots, rank):
    features = row.shape[2]
    packed = rank * LANES // features
    rollouts = index.shape[0] // dests
    rows = rollouts * rank + rollouts // 2 * packed
    return pl.pallas_call(
        functools.partial(pick_kernel, slots, rank),
        out_shape=jax.ShapeDtypeStruct((dests, rows, features), row.dtype),
        in_specs=[
            pl.BlockSpec(memory_space=pltpu.SMEM),
            pl.BlockSpec(memory_space=pltpu.VMEM),
        ],
        out_specs=pl.BlockSpec(memory_space=pltpu.VMEM),
        cost_estimate=cost(0, 2 * dests * rows * features),
        compiler_params=pltpu.CompilerParams(vmem_limit_bytes=KERNEL_VMEM),
        name="pick_factors",
    )(index, row)


def down_kernel(own_row_ref, hidden_ref, factor_ref, out_ref):
    members, rank, chunk = out_ref.shape
    count = own_row_ref.shape[0]
    per = members // count
    length = per * chunk
    for r in range(count):
        product = lax.dot_general(
            hidden_ref[r * length : (r + 1) * length],
            factor_ref[own_row_ref[r], r * rank : (r + 1) * rank],
            (((1,), (1,)), ((), ())),
            preferred_element_type=jnp.float32,
        ).T.astype(out_ref.dtype)
        for i in range(per):
            out_ref[r * per + i] = product[:, i * chunk : (i + 1) * chunk]


def down_projection(own_row, hidden, factors, members, rank):
    tokens, features = hidden.shape
    return pl.pallas_call(
        down_kernel,
        out_shape=jax.ShapeDtypeStruct((members, rank, tokens // members), hidden.dtype),
        in_specs=[pl.BlockSpec(memory_space=pltpu.SMEM)]
        + [pl.BlockSpec(memory_space=pltpu.VMEM)] * 2,
        out_specs=pl.BlockSpec(memory_space=pltpu.VMEM),
        cost_estimate=cost(2 * tokens * features * rank, hidden.size + tokens * rank),
        compiler_params=pltpu.CompilerParams(vmem_limit_bytes=KERNEL_VMEM),
        name="down_projection",
    )(own_row, hidden, factors)


def sum_kernel(parts_ref, out_ref):
    total = parts_ref[0].astype(jnp.float32)
    for i in range(1, parts_ref.shape[0]):
        total += parts_ref[i].astype(jnp.float32)
    total = total.astype(out_ref.dtype)
    for i in range(out_ref.shape[0]):
        out_ref[i] = total


def sum_copies(parts):
    return pl.pallas_call(
        sum_kernel,
        out_shape=jax.ShapeDtypeStruct(parts.shape, parts.dtype),
        in_specs=[pl.BlockSpec(memory_space=pltpu.VMEM)],
        out_specs=pl.BlockSpec(memory_space=pltpu.VMEM),
        cost_estimate=cost(parts.size, 2 * parts.size),
        compiler_params=pltpu.CompilerParams(vmem_limit_bytes=KERNEL_VMEM),
        name="sum_parts",
    )(parts)


def final_kernel(own_row_ref, lengths_ref, *refs):
    *base_refs, down_ref, factor_ref, out_ref = refs
    columns, tokens = out_ref.shape
    members, rank, chunk = down_ref.shape
    features = factor_ref.shape[2]
    packed = rank * LANES // features
    count = own_row_ref.shape[0]
    per, length = members // count, tokens // count
    for r in range(count):
        at = count * rank + r // 2 * packed
        block = factor_ref[own_row_ref[r], at : at + packed, :]
        first = r % 2 * columns
        up = jnp.concatenate(
            [
                block[:, q * LANES + first : q * LANES + first + columns]
                for q in range(features // LANES)
            ],
            axis=0,
        )
        down = jnp.concatenate([down_ref[r * per + i] for i in range(per)], axis=1)
        update = lax.dot_general(
            up, down, (((0,), (0,)), ((), ())), preferred_element_type=jnp.float32
        )
        span = slice(r * length, (r + 1) * length)
        total = ADAPTER_SCALE * update
        for base_ref in base_refs:
            total += base_ref[:, span].astype(jnp.float32)
        position = lax.broadcasted_iota(jnp.int32, (columns, length), 1)
        out_ref[:, span] = jnp.where(position < lengths_ref[r], total, 0.0).astype(out_ref.dtype)


def final(own_row, lengths, base, down, factors):
    columns, tokens = base[0].shape
    rank = down.shape[1]
    return pl.pallas_call(
        final_kernel,
        out_shape=jax.ShapeDtypeStruct(base[0].shape, base[0].dtype),
        in_specs=[pl.BlockSpec(memory_space=pltpu.SMEM)] * 2
        + [pl.BlockSpec(memory_space=pltpu.VMEM)] * (len(base) + 2),
        out_specs=pl.BlockSpec(memory_space=pltpu.VMEM),
        cost_estimate=cost(2 * tokens * columns * rank, 4 * base[0].size + down.size),
        compiler_params=pltpu.CompilerParams(vmem_limit_bytes=KERNEL_VMEM),
        name="add_update",
    )(own_row, lengths, *base, down, factors)


def on_device(
    hidden, value_matrix, adapter_down_store, adapter_up_store, adapter_slot, rollout_adapter, lengths
):
    members = lax.axis_size(TENSOR)
    rollouts = rollout_adapter.shape[0]
    slots_here, rank, _ = adapter_up_store.shape
    row_slots = slots_here * lax.axis_size("y")

    other = along("core", hidden, 1)
    other_matrix = along("core", value_matrix, 1)
    copies = factor_copies(
        jnp.swapaxes(adapter_down_store, 1, 2), adapter_up_store, lax.axis_size("y")
    )
    row = lax.all_to_all(copies, "y", 0, 0)

    parts = project(hidden, other, value_matrix, other_matrix, adapter_up_store.shape[2])
    *parts, rollout_adapter = lax.optimization_barrier((*parts, rollout_adapter))
    *parts, own, far = parts
    chain = vmem_call(add_own_kernel, "add_own", WEIGHTS[0], like(parts[0]), parts[0], hop(far))
    for i, part in enumerate(parts[1:], 1):
        chain = vmem_call(add_kernel, "add_parts", WEIGHTS[i], like(part), part, hop(chain))
    kept, sent = vmem_call(
        split_kernel, "split", WEIGHTS[-1], [like(own), like(own)], hop(chain), own
    )
    base = (kept, along("core", sent, 1))

    here = lax.axis_index("x")
    mine = jnp.arange(X, dtype=jnp.int32)[:, None] == here
    wanted = lax.psum(jnp.where(mine, rollout_adapter[None, :], 0), "x").reshape(-1)
    table = jnp.arange(adapter_slot.shape[0], dtype=jnp.int32)
    matches = wanted[:, None] == table[None, :]
    slots = jnp.sum(jnp.where(matches, adapter_slot[None, :], 0), axis=1)
    local = jnp.clip(slots - here * row_slots, 0, row_slots - 1)
    own_row = lax.dynamic_slice_in_dim(slots, here * rollouts, rollouts) // row_slots
    local, own_row = lax.optimization_barrier((local, own_row))

    sent = pick(local, row, X, slots_here, rank)
    factors = lax.all_to_all(sent, "x", 0, 0)
    down = down_projection(own_row, hidden, factors, members, rank)
    down = lax.all_to_all(down, TENSOR, 0, 0)
    down = sum_copies(down)
    down = lax.all_to_all(down, TENSOR, 0, 0)
    return final(own_row, lengths, base, down, factors).T


def solution(mesh):
    dp, tensor = mesh.devices.shape
    fine = Mesh(mesh.devices.reshape(X, dp // X, tensor // CORES, CORES), (*DP, *TENSOR))
    in_specs = (
        P(DP, TENSOR),
        P(TENSOR, None),
        P(DP, TENSOR, None),
        P(DP, None, TENSOR),
        P(),
        P(DP),
        P(DP),
    )
    return jax.shard_map(
        on_device, mesh=fine, in_specs=in_specs, out_specs=P(DP, TENSOR), check_vma=False
    )
```

```python
import functools

import jax
import jax.numpy as jnp
from jax import lax
from jax.experimental import pallas as pl
from jax.experimental.pallas import tpu as pltpu
from jax.sharding import Mesh
from jax.sharding import PartitionSpec as P

ADAPTER_SCALE = 2.0
X, CORES = 4, 2
DP, TENSOR = ("x", "y"), ("z", "core")
LANES = 128
WEIGHTS = (1, 1, 1, 50000, 1)
KERNEL_VMEM = 8 << 20
PROJECT_VMEM, PROJECT_PARTS = 60 << 20, 2


def cost(flops, size):
    return pl.CostEstimate(flops=flops, bytes_accessed=2 * size, transcendentals=0)


def copies_kernel(down_ref, up_ref, out_ref, stage, ups, in_sems, sems):
    slots, rank, features = down_ref.shape
    packed = stage.shape[0] - slots * rank
    first = [
        pltpu.make_async_copy(down_ref.at[j], stage.at[pl.ds(j * rank, rank)], in_sems.at[j])
        for j in range(slots)
    ]
    first.append(pltpu.make_async_copy(up_ref, ups, in_sems.at[slots]))
    copies = [
        pltpu.make_async_copy(stage, out_ref.at[i], sems.at[i]) for i in range(out_ref.shape[0])
    ]
    for copy in first:
        copy.start()
    for copy in first:
        copy.wait()
    both = jnp.concatenate([ups[j] for j in range(slots)], axis=1)
    for q in range(features // LANES):
        block = both[q * packed : (q + 1) * packed]
        stage[slots * rank :, q * LANES : (q + 1) * LANES] = block
    for copy in copies:
        copy.start()
    for copy in copies:
        copy.wait()


def factor_copies(down, up, count):
    slots, rank, features = down.shape
    rows = slots * rank + rank * LANES // features
    return pl.pallas_call(
        copies_kernel,
        out_shape=jax.ShapeDtypeStruct((count, rows, features), down.dtype),
        in_specs=[pl.BlockSpec(memory_space=pl.ANY)] * 2,
        out_specs=pl.BlockSpec(memory_space=pl.ANY),
        scratch_shapes=[
            pltpu.VMEM((rows, features), down.dtype),
            pltpu.VMEM(up.shape, up.dtype),
            pltpu.SemaphoreType.DMA((slots + 1,)),
            pltpu.SemaphoreType.DMA((count,)),
        ],
        cost_estimate=cost(0, count * rows * features),
        compiler_params=pltpu.CompilerParams(vmem_limit_bytes=PROJECT_VMEM),
        name="factor_copies",
    )(down, up)


def project_kernel(hidden_ref, matrix_ref, *refs):
    *out_refs, mine, whole, chosen, stage, in_sems, out_sems = refs
    near_ref, middle_ref = out_refs[:2]
    span = middle_ref.shape[0] // 2
    columns = span // CORES
    chips = whole.shape[1] // span
    tokens = mine.shape[0]
    rows = tokens // PROJECT_PARTS

    take = [pltpu.make_async_copy(matrix_ref, whole, in_sems.at[0])] + [
        pltpu.make_async_copy(
            hidden_ref.at[pl.ds(i * rows, rows)], mine.at[pl.ds(i * rows, rows)], in_sems.at[1 + i]
        )
        for i in range(PROJECT_PARTS)
    ]
    for copy in take:
        copy.start()

    here = lax.axis_index("z")
    low = lax.broadcasted_iota(jnp.int32, (whole.shape[0], span), 1) < columns

    def block(chip):
        start = pl.multiple_of(lax.rem(chip + chips, chips) * span, span)
        return whole[:, pl.ds(start, span)]

    def turned(value):
        return jnp.concatenate([value[:, columns:], value[:, :columns]], axis=1)

    take[0].wait()
    for core, flip in enumerate((True, False)):
        upper = (lax.axis_index("core") == 1) != flip
        own, far = block(here), block(here + chips // 2)
        own = jnp.where(upper, turned(own), own)
        far = jnp.where(upper, far, turned(far))
        chosen[2 * core, :, :span] = block(here + jnp.where(upper, -3, 3))
        chosen[2 * core, :, span:] = jnp.where(low, own, far)
        chosen[2 * core + 1, :, :span] = block(here + jnp.where(upper, -2, 2))
        chosen[2 * core + 1, :, span:] = block(here + jnp.where(upper, -1, 1))

    places = [
        [(near_ref, 0)],
        [(middle_ref, 0)],
        [(out_refs[2], 0), (out_refs[5], span), (out_refs[6], span + columns)],
        [(out_refs[3], 0), (out_refs[4], span)],
    ]
    leave = []
    for g, group in enumerate(places):
        for i in range(PROJECT_PARTS):
            if g == 0:
                take[1 + i].wait()
            part = slice(i * rows, (i + 1) * rows)
            product = jnp.dot(mine[part], chosen[g], preferred_element_type=jnp.float32)
            stage[g, :, part] = product.astype(stage.dtype).T
        for ref, start in group:
            copy = pltpu.make_async_copy(
                stage.at[g, pl.ds(start, ref.shape[0])], ref, out_sems.at[len(leave)]
            )
            copy.start()
            leave.append(copy)
    for copy in leave:
        copy.wait()


def project(hidden, matrix, columns):
    tokens, features = hidden.shape
    kind = hidden.dtype
    span = CORES * columns
    heights = [2 * span] * 2 + [span] * 3 + [columns] * 2
    anywhere = pl.BlockSpec(memory_space=pl.ANY)
    return pl.pallas_call(
        project_kernel,
        out_shape=[jax.ShapeDtypeStruct((height, tokens), kind) for height in heights],
        in_specs=[anywhere] * 2,
        out_specs=[anywhere] * len(heights),
        scratch_shapes=[
            pltpu.VMEM(hidden.shape, kind),
            pltpu.VMEM(matrix.shape, kind),
            pltpu.VMEM((4, features, 2 * span), kind),
            pltpu.VMEM((4, 2 * span, tokens), kind),
            pltpu.SemaphoreType.DMA((1 + PROJECT_PARTS,)),
            pltpu.SemaphoreType.DMA((len(heights),)),
        ],
        cost_estimate=cost(0, 0),
        compiler_params=pltpu.CompilerParams(vmem_limit_bytes=PROJECT_VMEM),
        name="project",
    )(hidden, matrix)


def vmem_call(kernel, name, weight, out_shape, *operands):
    size = operands[0].size
    several = isinstance(out_shape, list)
    spec = pl.BlockSpec(memory_space=pltpu.VMEM)
    return pl.pallas_call(
        kernel,
        out_shape=out_shape,
        in_specs=[spec] * len(operands),
        out_specs=[spec] * len(out_shape) if several else spec,
        cost_estimate=cost(weight * size, 3 * size),
        compiler_params=pltpu.CompilerParams(vmem_limit_bytes=KERNEL_VMEM),
        name=name,
    )(*operands)


def like(value, rows=None):
    return jax.ShapeDtypeStruct((rows or value.shape[0], *value.shape[1:]), value.dtype)


def sum_refs(*values):
    total = values[0].astype(jnp.float32)
    for value in values[1:]:
        total += value.astype(jnp.float32)
    return total.astype(values[0].dtype)


def add_kernel(first, part_ref, other_ref, came_ref, out_ref):
    other = other_ref[first : first + part_ref.shape[0]]
    out_ref[...] = sum_refs(part_ref[...], other, came_ref[...])


def add_far_kernel(first, part_ref, other_ref, out_ref):
    out_ref[...] = sum_refs(part_ref[...], other_ref[first : first + part_ref.shape[0]])


def add_own_kernel(first, part_ref, other_ref, came_ref, out_ref):
    columns = came_ref.shape[0]
    core = lax.axis_index("core")
    mine = pl.ds(pl.multiple_of(core * columns, columns), columns)
    out_ref[...] = sum_refs(part_ref[...], other_ref[first : first + part_ref.shape[0]])
    out_ref[mine] = sum_refs(out_ref[mine], came_ref[...])


def split_kernel(first, own_ref, other_ref, chain_ref, kept_ref, sent_ref):
    columns = own_ref.shape[0]
    core = lax.axis_index("core")
    mine = pl.ds(pl.multiple_of(core * columns, columns), columns)
    theirs = pl.ds(pl.multiple_of((1 - core) * columns, columns), columns)
    other = other_ref[first : first + columns]
    kept_ref[...] = sum_refs(own_ref[...], other, chain_ref[mine])
    sent_ref[...] = chain_ref[theirs]


def hop(value):
    n = lax.axis_size("z")
    pairs = [
        (z * CORES + core, (z + (1 - 2 * core)) % n * CORES + core)
        for z in range(n)
        for core in range(CORES)
    ]
    return lax.ppermute(value, TENSOR, pairs)


def along(axis, value, step):
    n = lax.axis_size(axis)
    return lax.ppermute(value, axis, [(i, (i + step) % n) for i in range(n)])


def pick_kernel(slots, rank, index_ref, row_ref, out_ref):
    dests, _, features = out_ref.shape
    packed = rank * LANES // features
    rollouts = index_ref.shape[0] // dests
    half = LANES // 2
    low = lax.broadcasted_iota(jnp.int32, (packed, LANES), 1) < half
    for d in range(dests):
        ups = []
        for r in range(rollouts):
            index = index_ref[d * rollouts + r]
            owner, place = index // slots, index % slots
            start = pl.multiple_of(place * rank, rank)
            out_ref[d, r * rank : (r + 1) * rank] = row_ref[owner, pl.ds(start, rank)]
            ups.append((row_ref[owner, slots * rank :], place))
        for p in range(rollouts // 2):
            for q in range(features // LANES):
                lanes = slice(q * LANES, (q + 1) * LANES)
                pair = []
                for h in range(2):
                    block, place = ups[2 * p + h]
                    block = block[:, lanes]
                    turned = jnp.concatenate([block[:, half:], block[:, :half]], axis=1)
                    pair.append(jnp.where(place == h, block, turned))
                at = rollouts * rank + p * packed
                out_ref[d, at : at + packed, lanes] = jnp.where(low, pair[0], pair[1])


def pick(index, row, dests, slots, rank):
    features = row.shape[2]
    packed = rank * LANES // features
    rollouts = index.shape[0] // dests
    rows = rollouts * rank + rollouts // 2 * packed
    return pl.pallas_call(
        functools.partial(pick_kernel, slots, rank),
        out_shape=jax.ShapeDtypeStruct((dests, rows, features), row.dtype),
        in_specs=[
            pl.BlockSpec(memory_space=pltpu.SMEM),
            pl.BlockSpec(memory_space=pltpu.VMEM),
        ],
        out_specs=pl.BlockSpec(memory_space=pltpu.VMEM),
        cost_estimate=cost(0, 2 * dests * rows * features),
        compiler_params=pltpu.CompilerParams(vmem_limit_bytes=KERNEL_VMEM),
        name="pick_factors",
    )(index, row)


def down_kernel(own_row_ref, hidden_ref, factor_ref, out_ref, up_ref):
    members, rank, chunk = out_ref.shape
    packed = up_ref.shape[1]
    count = own_row_ref.shape[0]
    per = members // count
    length = per * chunk
    for r in range(count):
        product = lax.dot_general(
            hidden_ref[r * length : (r + 1) * length],
            factor_ref[own_row_ref[r], r * rank : (r + 1) * rank],
            (((1,), (1,)), ((), ())),
            preferred_element_type=jnp.float32,
        ).T.astype(out_ref.dtype)
        for i in range(per):
            out_ref[r * per + i] = product[:, i * chunk : (i + 1) * chunk]
        at = count * rank + r // 2 * packed
        up_ref[r] = factor_ref[own_row_ref[r], at : at + packed]


def down_projection(own_row, hidden, factors, members, rank):
    tokens, features = hidden.shape
    packed = rank * LANES // features
    return pl.pallas_call(
        down_kernel,
        out_shape=[
            jax.ShapeDtypeStruct((members, rank, tokens // members), hidden.dtype),
            jax.ShapeDtypeStruct((own_row.shape[0], packed, features), factors.dtype),
        ],
        in_specs=[pl.BlockSpec(memory_space=pltpu.SMEM)]
        + [pl.BlockSpec(memory_space=pltpu.VMEM)] * 2,
        out_specs=[pl.BlockSpec(memory_space=pltpu.VMEM)] * 2,
        cost_estimate=cost(2 * tokens * features * rank, hidden.size + tokens * rank),
        compiler_params=pltpu.CompilerParams(vmem_limit_bytes=KERNEL_VMEM),
        name="down_projection",
    )(own_row, hidden, factors)


def sum_kernel(parts_ref, out_ref):
    total = parts_ref[0].astype(jnp.float32)
    for i in range(1, parts_ref.shape[0]):
        total += parts_ref[i].astype(jnp.float32)
    total = total.astype(out_ref.dtype)
    for i in range(out_ref.shape[0]):
        out_ref[i] = total


def sum_copies(parts):
    return pl.pallas_call(
        sum_kernel,
        out_shape=jax.ShapeDtypeStruct(parts.shape, parts.dtype),
        in_specs=[pl.BlockSpec(memory_space=pltpu.VMEM)],
        out_specs=pl.BlockSpec(memory_space=pltpu.VMEM),
        cost_estimate=cost(parts.size, 2 * parts.size),
        compiler_params=pltpu.CompilerParams(vmem_limit_bytes=KERNEL_VMEM),
        name="sum_parts",
    )(parts)


def final_kernel(lengths_ref, *refs):
    *base_refs, down_ref, up_ref, out_ref = refs
    columns, tokens = out_ref.shape
    members, rank, chunk = down_ref.shape
    count, _, features = up_ref.shape
    per, length = members // count, tokens // count
    for r in range(count):
        block = up_ref[r]
        first = r % 2 * columns
        up = jnp.concatenate(
            [
                block[:, q * LANES + first : q * LANES + first + columns]
                for q in range(features // LANES)
            ],
            axis=0,
        )
        down = jnp.concatenate([down_ref[r * per + i] for i in range(per)], axis=1)
        update = lax.dot_general(
            up, down, (((0,), (0,)), ((), ())), preferred_element_type=jnp.float32
        )
        span = slice(r * length, (r + 1) * length)
        total = ADAPTER_SCALE * update
        for base_ref in base_refs:
            total += base_ref[:, span].astype(jnp.float32)
        position = lax.broadcasted_iota(jnp.int32, (columns, length), 1)
        out_ref[:, span] = jnp.where(position < lengths_ref[r], total, 0.0).astype(out_ref.dtype)


def final(lengths, base, down, ups):
    columns, tokens = base[0].shape
    rank = down.shape[1]
    return pl.pallas_call(
        final_kernel,
        out_shape=jax.ShapeDtypeStruct(base[0].shape, base[0].dtype),
        in_specs=[pl.BlockSpec(memory_space=pltpu.SMEM)]
        + [pl.BlockSpec(memory_space=pltpu.VMEM)] * (len(base) + 2),
        out_specs=pl.BlockSpec(memory_space=pltpu.VMEM),
        cost_estimate=cost(2 * tokens * columns * rank, 4 * base[0].size + down.size),
        compiler_params=pltpu.CompilerParams(vmem_limit_bytes=KERNEL_VMEM),
        name="add_update",
    )(lengths, *base, down, ups)


def on_device(
    hidden, value_matrix, adapter_down_store, adapter_up_store, adapter_slot, rollout_adapter, lengths
):
    members = lax.axis_size(TENSOR)
    rollouts = rollout_adapter.shape[0]
    slots_here, rank, _ = adapter_up_store.shape
    row_slots = slots_here * lax.axis_size("y")

    copies = factor_copies(
        jnp.swapaxes(adapter_down_store, 1, 2), adapter_up_store, lax.axis_size("y")
    )
    row = lax.all_to_all(copies, "y", 0, 0)

    columns = adapter_up_store.shape[2]
    span = CORES * columns
    near, middle, *parts, own, far = project(hidden, value_matrix, columns)
    near, middle = along("core", near, 1), along("core", middle, 1)
    *parts, own, far, rollout_adapter = lax.optimization_barrier((*parts, own, far, rollout_adapter))

    def add(kernel, first, weight, name, part, *others):
        return vmem_call(functools.partial(kernel, first), name, weight, like(part), part, *others)

    chain = add(add_far_kernel, span + columns, WEIGHTS[0], "add_far", far, near)
    chain = add(add_own_kernel, 0, WEIGHTS[1], "add_own", parts[0], near, hop(chain))
    chain = add(add_kernel, 0, WEIGHTS[2], "add_parts", parts[1], middle, hop(chain))
    chain = add(add_kernel, span, WEIGHTS[3], "add_parts", parts[2], middle, hop(chain))
    kept, sent = vmem_call(
        functools.partial(split_kernel, span),
        "split",
        WEIGHTS[4],
        [like(own), like(own)],
        own,
        near,
        hop(chain),
    )
    base = (kept, along("core", sent, 1))

    here = lax.axis_index("x")
    mine = jnp.arange(X, dtype=jnp.int32)[:, None] == here
    wanted = lax.psum(jnp.where(mine, rollout_adapter[None, :], 0), "x").reshape(-1)
    table = jnp.arange(adapter_slot.shape[0], dtype=jnp.int32)
    matches = wanted[:, None] == table[None, :]
    slots = jnp.sum(jnp.where(matches, adapter_slot[None, :], 0), axis=1)
    local = jnp.clip(slots - here * row_slots, 0, row_slots - 1)
    own_row = lax.dynamic_slice_in_dim(slots, here * rollouts, rollouts) // row_slots
    local, own_row = lax.optimization_barrier((local, own_row))

    sent = pick(local, row, X, slots_here, rank)
    factors = lax.all_to_all(sent, "x", 0, 0)
    down, ups = down_projection(own_row, hidden, factors, members, rank)
    down = lax.all_to_all(down, TENSOR, 0, 0)
    down = sum_copies(down)
    down = lax.all_to_all(down, TENSOR, 0, 0)
    return final(lengths, base, down, ups).T


def solution(mesh):
    dp, tensor = mesh.devices.shape
    fine = Mesh(mesh.devices.reshape(X, dp // X, tensor // CORES, CORES), (*DP, *TENSOR))
    in_specs = (
        P(DP, TENSOR),
        P(TENSOR, None),
        P(DP, TENSOR, None),
        P(DP, None, TENSOR),
        P(),
        P(DP),
        P(DP),
    )
    return jax.shard_map(
        on_device, mesh=fine, in_specs=in_specs, out_specs=P(DP, TENSOR), check_vma=False
    )
```

```python
import functools

import jax
import jax.numpy as jnp
from jax import lax
from jax.experimental import pallas as pl
from jax.experimental.pallas import tpu as pltpu
from jax.sharding import Mesh
from jax.sharding import PartitionSpec as P

ADAPTER_SCALE = 2.0
X, CORES = 4, 2
DP, TENSOR = ("x", "y"), ("z", "core")
LANES = 128
WEIGHTS = (1, 1, 1, 50000, 1)
KERNEL_VMEM, COPIES_VMEM = 8 << 20, 60 << 20
PROJECT_VMEM, PROJECT_PARTS = 60 << 20, 2


def cost(flops, size):
    return pl.CostEstimate(flops=flops, bytes_accessed=2 * size, transcendentals=0)


def copies_kernel(down_ref, up_ref, out_ref, stage, ups, in_sems, sems):
    slots, rank, features = down_ref.shape
    packed = stage.shape[0] - slots * rank
    first = [
        pltpu.make_async_copy(down_ref.at[j], stage.at[pl.ds(j * rank, rank)], in_sems.at[j])
        for j in range(slots)
    ]
    first.append(pltpu.make_async_copy(up_ref, ups, in_sems.at[slots]))
    copies = [
        pltpu.make_async_copy(stage, out_ref.at[i], sems.at[i]) for i in range(out_ref.shape[0])
    ]
    for copy in first:
        copy.start()
    for copy in first:
        copy.wait()
    both = jnp.concatenate([ups[j] for j in range(slots)], axis=1)
    for q in range(features // LANES):
        block = both[q * packed : (q + 1) * packed]
        stage[slots * rank :, q * LANES : (q + 1) * LANES] = block
    for copy in copies:
        copy.start()
    for copy in copies:
        copy.wait()


def factor_copies(down, up, count):
    slots, rank, features = down.shape
    rows = slots * rank + rank * LANES // features
    return pl.pallas_call(
        copies_kernel,
        out_shape=jax.ShapeDtypeStruct((count, rows, features), down.dtype),
        in_specs=[pl.BlockSpec(memory_space=pl.ANY)] * 2,
        out_specs=pl.BlockSpec(memory_space=pl.ANY),
        scratch_shapes=[
            pltpu.VMEM((rows, features), down.dtype),
            pltpu.VMEM(up.shape, up.dtype),
            pltpu.SemaphoreType.DMA((slots + 1,)),
            pltpu.SemaphoreType.DMA((count,)),
        ],
        cost_estimate=cost(0, count * rows * features),
        compiler_params=pltpu.CompilerParams(vmem_limit_bytes=PROJECT_VMEM),
        name="factor_copies",
    )(down, up)


def project_kernel(hidden_ref, matrix_ref, *refs):
    *out_refs, mine, whole, chosen, stage, in_sems, out_sems = refs
    near_ref, middle_ref = out_refs[:2]
    span = middle_ref.shape[0] // 2
    columns = span // CORES
    chips = whole.shape[1] // span
    tokens = mine.shape[0]
    rows = tokens // PROJECT_PARTS

    take = [pltpu.make_async_copy(matrix_ref, whole, in_sems.at[0])] + [
        pltpu.make_async_copy(
            hidden_ref.at[pl.ds(i * rows, rows)], mine.at[pl.ds(i * rows, rows)], in_sems.at[1 + i]
        )
        for i in range(PROJECT_PARTS)
    ]
    for copy in take:
        copy.start()

    here = lax.axis_index("z")
    low = lax.broadcasted_iota(jnp.int32, (whole.shape[0], span), 1) < columns

    def block(chip):
        start = pl.multiple_of(lax.rem(chip + chips, chips) * span, span)
        return whole[:, pl.ds(start, span)]

    def turned(value):
        return jnp.concatenate([value[:, columns:], value[:, :columns]], axis=1)

    take[0].wait()
    for core, flip in enumerate((True, False)):
        upper = (lax.axis_index("core") == 1) != flip
        own, far = block(here), block(here + chips // 2)
        own = jnp.where(upper, turned(own), own)
        far = jnp.where(upper, far, turned(far))
        chosen[2 * core, :, :span] = block(here + jnp.where(upper, -3, 3))
        chosen[2 * core, :, span:] = jnp.where(low, own, far)
        chosen[2 * core + 1, :, :span] = block(here + jnp.where(upper, -2, 2))
        chosen[2 * core + 1, :, span:] = block(here + jnp.where(upper, -1, 1))

    places = [
        [(near_ref, 0)],
        [(middle_ref, 0)],
        [(out_refs[2], 0), (out_refs[5], span), (out_refs[6], span + columns)],
        [(out_refs[3], 0), (out_refs[4], span)],
    ]
    leave = []
    for g, group in enumerate(places):
        for i in range(PROJECT_PARTS):
            if g == 0:
                take[1 + i].wait()
            part = slice(i * rows, (i + 1) * rows)
            product = jnp.dot(mine[part], chosen[g], preferred_element_type=jnp.float32)
            stage[g, :, part] = product.astype(stage.dtype).T
        for ref, start in group:
            copy = pltpu.make_async_copy(
                stage.at[g, pl.ds(start, ref.shape[0])], ref, out_sems.at[len(leave)]
            )
            copy.start()
            leave.append(copy)
    for copy in leave:
        copy.wait()


def project(hidden, matrix, columns):
    tokens, features = hidden.shape
    kind = hidden.dtype
    span = CORES * columns
    heights = [2 * span] * 2 + [span] * 3 + [columns] * 2
    anywhere = pl.BlockSpec(memory_space=pl.ANY)
    return pl.pallas_call(
        project_kernel,
        out_shape=[jax.ShapeDtypeStruct((height, tokens), kind) for height in heights],
        in_specs=[anywhere] * 2,
        out_specs=[anywhere] * len(heights),
        scratch_shapes=[
            pltpu.VMEM(hidden.shape, kind),
            pltpu.VMEM(matrix.shape, kind),
            pltpu.VMEM((4, features, 2 * span), kind),
            pltpu.VMEM((4, 2 * span, tokens), kind),
            pltpu.SemaphoreType.DMA((1 + PROJECT_PARTS,)),
            pltpu.SemaphoreType.DMA((len(heights),)),
        ],
        cost_estimate=cost(0, 0),
        compiler_params=pltpu.CompilerParams(vmem_limit_bytes=PROJECT_VMEM),
        name="project",
    )(hidden, matrix)


def vmem_call(kernel, name, weight, out_shape, *operands):
    size = operands[0].size
    several = isinstance(out_shape, list)
    spec = pl.BlockSpec(memory_space=pltpu.VMEM)
    return pl.pallas_call(
        kernel,
        out_shape=out_shape,
        in_specs=[spec] * len(operands),
        out_specs=[spec] * len(out_shape) if several else spec,
        cost_estimate=cost(weight * size, 3 * size),
        compiler_params=pltpu.CompilerParams(vmem_limit_bytes=COPIES_VMEM if name == "add_parts" else KERNEL_VMEM),
        name=name,
    )(*operands)


def like(value, rows=None):
    return jax.ShapeDtypeStruct((rows or value.shape[0], *value.shape[1:]), value.dtype)


def sum_refs(*values):
    total = values[0].astype(jnp.float32)
    for value in values[1:]:
        total += value.astype(jnp.float32)
    return total.astype(values[0].dtype)


def add_kernel(first, part_ref, other_ref, came_ref, out_ref):
    other = other_ref[first : first + part_ref.shape[0]]
    out_ref[...] = sum_refs(part_ref[...], other, came_ref[...])


def add_far_kernel(first, far_ref, own_ref, other_ref, far_out_ref, own_out_ref):
    columns = own_ref.shape[0]
    own_out_ref[...] = sum_refs(own_ref[...], other_ref[first : first + columns])
    far_out_ref[...] = sum_refs(far_ref[...], other_ref[first + columns : first + 2 * columns])


def add_own_kernel(first, part_ref, other_ref, came_ref, out_ref):
    columns = came_ref.shape[0]
    core = lax.axis_index("core")
    mine = pl.ds(pl.multiple_of(core * columns, columns), columns)
    out_ref[...] = sum_refs(part_ref[...], other_ref[first : first + part_ref.shape[0]])
    out_ref[mine] = sum_refs(out_ref[mine], came_ref[...])


def split_kernel(own_ref, chain_ref, kept_ref, sent_ref):
    columns = own_ref.shape[0]
    core = lax.axis_index("core")
    mine = pl.ds(pl.multiple_of(core * columns, columns), columns)
    theirs = pl.ds(pl.multiple_of((1 - core) * columns, columns), columns)
    kept_ref[...] = sum_refs(own_ref[...], chain_ref[mine])
    sent_ref[...] = chain_ref[theirs]


def hop(value):
    n = lax.axis_size("z")
    pairs = [
        (z * CORES + core, (z + (1 - 2 * core)) % n * CORES + core)
        for z in range(n)
        for core in range(CORES)
    ]
    return lax.ppermute(value, TENSOR, pairs)


def along(axis, value, step):
    n = lax.axis_size(axis)
    return lax.ppermute(value, axis, [(i, (i + step) % n) for i in range(n)])


def pick_kernel(slots, rank, index_ref, row_ref, out_ref):
    dests, _, features = out_ref.shape
    packed = rank * LANES // features
    rollouts = index_ref.shape[0] // dests
    half = LANES // 2
    low = lax.broadcasted_iota(jnp.int32, (packed, LANES), 1) < half
    for d in range(dests):
        ups = []
        for r in range(rollouts):
            index = index_ref[d * rollouts + r]
            owner, place = index // slots, index % slots
            start = pl.multiple_of(place * rank, rank)
            out_ref[d, r * rank : (r + 1) * rank] = row_ref[owner, pl.ds(start, rank)]
            ups.append((row_ref[owner, slots * rank :], place))
        for p in range(rollouts // 2):
            for q in range(features // LANES):
                lanes = slice(q * LANES, (q + 1) * LANES)
                pair = []
                for h in range(2):
                    block, place = ups[2 * p + h]
                    block = block[:, lanes]
                    turned = jnp.concatenate([block[:, half:], block[:, :half]], axis=1)
                    pair.append(jnp.where(place == h, block, turned))
                at = rollouts * rank + p * packed
                out_ref[d, at : at + packed, lanes] = jnp.where(low, pair[0], pair[1])


def pick(index, row, dests, slots, rank):
    features = row.shape[2]
    packed = rank * LANES // features
    rollouts = index.shape[0] // dests
    rows = rollouts * rank + rollouts // 2 * packed
    return pl.pallas_call(
        functools.partial(pick_kernel, slots, rank),
        out_shape=jax.ShapeDtypeStruct((dests, rows, features), row.dtype),
        in_specs=[
            pl.BlockSpec(memory_space=pltpu.SMEM),
            pl.BlockSpec(memory_space=pltpu.VMEM),
        ],
        out_specs=pl.BlockSpec(memory_space=pltpu.VMEM),
        cost_estimate=cost(0, 2 * dests * rows * features),
        compiler_params=pltpu.CompilerParams(vmem_limit_bytes=KERNEL_VMEM),
        name="pick_factors",
    )(index, row)


def down_kernel(own_row_ref, hidden_ref, factor_ref, out_ref, up_ref):
    members, rank, chunk = out_ref.shape
    packed = up_ref.shape[1]
    count = own_row_ref.shape[0]
    per = members // count
    length = per * chunk
    for r in range(count):
        product = lax.dot_general(
            hidden_ref[r * length : (r + 1) * length],
            factor_ref[own_row_ref[r], r * rank : (r + 1) * rank],
            (((1,), (1,)), ((), ())),
            preferred_element_type=jnp.float32,
        ).T.astype(out_ref.dtype)
        for i in range(per):
            out_ref[r * per + i] = product[:, i * chunk : (i + 1) * chunk]
        at = count * rank + r // 2 * packed
        up_ref[r] = factor_ref[own_row_ref[r], at : at + packed]


def down_projection(own_row, hidden, factors, members, rank):
    tokens, features = hidden.shape
    packed = rank * LANES // features
    return pl.pallas_call(
        down_kernel,
        out_shape=[
            jax.ShapeDtypeStruct((members, rank, tokens // members), hidden.dtype),
            jax.ShapeDtypeStruct((own_row.shape[0], packed, features), factors.dtype),
        ],
        in_specs=[pl.BlockSpec(memory_space=pltpu.SMEM)]
        + [pl.BlockSpec(memory_space=pltpu.VMEM)] * 2,
        out_specs=[pl.BlockSpec(memory_space=pltpu.VMEM)] * 2,
        cost_estimate=cost(2 * tokens * features * rank, hidden.size + tokens * rank),
        compiler_params=pltpu.CompilerParams(vmem_limit_bytes=KERNEL_VMEM),
        name="down_projection",
    )(own_row, hidden, factors)


def sum_kernel(parts_ref, out_ref):
    total = parts_ref[0].astype(jnp.float32)
    for i in range(1, parts_ref.shape[0]):
        total += parts_ref[i].astype(jnp.float32)
    total = total.astype(out_ref.dtype)
    for i in range(out_ref.shape[0]):
        out_ref[i] = total


def sum_copies(parts):
    return pl.pallas_call(
        sum_kernel,
        out_shape=jax.ShapeDtypeStruct(parts.shape, parts.dtype),
        in_specs=[pl.BlockSpec(memory_space=pltpu.VMEM)],
        out_specs=pl.BlockSpec(memory_space=pltpu.VMEM),
        cost_estimate=cost(parts.size, 2 * parts.size),
        compiler_params=pltpu.CompilerParams(vmem_limit_bytes=KERNEL_VMEM),
        name="sum_parts",
    )(parts)


def final_kernel(lengths_ref, *refs):
    *base_refs, down_ref, up_ref, out_ref = refs
    columns, tokens = out_ref.shape
    members, rank, chunk = down_ref.shape
    count, _, features = up_ref.shape
    per, length = members // count, tokens // count
    for r in range(count):
        block = up_ref[r]
        first = r % 2 * columns
        up = jnp.concatenate(
            [
                block[:, q * LANES + first : q * LANES + first + columns]
                for q in range(features // LANES)
            ],
            axis=0,
        )
        down = jnp.concatenate([down_ref[r * per + i] for i in range(per)], axis=1)
        update = lax.dot_general(
            up, down, (((0,), (0,)), ((), ())), preferred_element_type=jnp.float32
        )
        span = slice(r * length, (r + 1) * length)
        total = ADAPTER_SCALE * update
        for base_ref in base_refs:
            total += base_ref[:, span].astype(jnp.float32)
        position = lax.broadcasted_iota(jnp.int32, (columns, length), 1)
        out_ref[:, span] = jnp.where(position < lengths_ref[r], total, 0.0).astype(out_ref.dtype)


def final(lengths, base, down, ups):
    columns, tokens = base[0].shape
    rank = down.shape[1]
    return pl.pallas_call(
        final_kernel,
        out_shape=jax.ShapeDtypeStruct(base[0].shape, base[0].dtype),
        in_specs=[pl.BlockSpec(memory_space=pltpu.SMEM)]
        + [pl.BlockSpec(memory_space=pltpu.VMEM)] * (len(base) + 2),
        out_specs=pl.BlockSpec(memory_space=pltpu.VMEM),
        cost_estimate=cost(2 * tokens * columns * rank, 4 * base[0].size + down.size),
        compiler_params=pltpu.CompilerParams(vmem_limit_bytes=KERNEL_VMEM),
        name="add_update",
    )(lengths, *base, down, ups)


def on_device(
    hidden, value_matrix, adapter_down_store, adapter_up_store, adapter_slot, rollout_adapter, lengths
):
    members = lax.axis_size(TENSOR)
    rollouts = rollout_adapter.shape[0]
    slots_here, rank, _ = adapter_up_store.shape
    row_slots = slots_here * lax.axis_size("y")

    copies = factor_copies(
        jnp.swapaxes(adapter_down_store, 1, 2), adapter_up_store, lax.axis_size("y")
    )
    row = lax.all_to_all(copies, "y", 0, 0)

    columns = adapter_up_store.shape[2]
    span = CORES * columns
    near, middle, *parts, own, far = project(hidden, value_matrix, columns)
    near, middle = along("core", near, 1), along("core", middle, 1)
    *parts, own, far, rollout_adapter = lax.optimization_barrier((*parts, own, far, rollout_adapter))

    def add(kernel, first, weight, name, part, *others):
        return vmem_call(functools.partial(kernel, first), name, weight, like(part), part, *others)

    chain, own = vmem_call(
        functools.partial(add_far_kernel, span),
        "add_far",
        WEIGHTS[0],
        [like(far), like(own)],
        far,
        own,
        near,
    )
    chain = add(add_own_kernel, 0, WEIGHTS[1], "add_own", parts[0], near, hop(chain))
    chain = add(add_kernel, 0, WEIGHTS[2], "add_parts", parts[1], middle, hop(chain))
    chain = add(add_kernel, span, WEIGHTS[3], "add_parts", parts[2], middle, hop(chain))
    kept, sent = vmem_call(
        split_kernel, "split", WEIGHTS[4], [like(own), like(own)], own, hop(chain)
    )
    base = (kept, along("core", sent, 1))

    here = lax.axis_index("x")
    mine = jnp.arange(X, dtype=jnp.int32)[:, None] == here
    wanted = lax.psum(jnp.where(mine, rollout_adapter[None, :], 0), "x").reshape(-1)
    table = jnp.arange(adapter_slot.shape[0], dtype=jnp.int32)
    matches = wanted[:, None] == table[None, :]
    slots = jnp.sum(jnp.where(matches, adapter_slot[None, :], 0), axis=1)
    local = jnp.clip(slots - here * row_slots, 0, row_slots - 1)
    own_row = lax.dynamic_slice_in_dim(slots, here * rollouts, rollouts) // row_slots
    local, own_row = lax.optimization_barrier((local, own_row))

    sent = pick(local, row, X, slots_here, rank)
    factors = lax.all_to_all(sent, "x", 0, 0)
    down, ups = down_projection(own_row, hidden, factors, members, rank)
    down = lax.all_to_all(down, TENSOR, 0, 0)
    down = sum_copies(down)
    down = lax.all_to_all(down, TENSOR, 0, 0)
    return final(lengths, base, down, ups).T


def solution(mesh):
    dp, tensor = mesh.devices.shape
    fine = Mesh(mesh.devices.reshape(X, dp // X, tensor // CORES, CORES), (*DP, *TENSOR))
    in_specs = (
        P(DP, TENSOR),
        P(TENSOR, None),
        P(DP, TENSOR, None),
        P(DP, None, TENSOR),
        P(),
        P(DP),
        P(DP),
    )
    return jax.shard_map(
        on_device, mesh=fine, in_specs=in_specs, out_specs=P(DP, TENSOR), check_vma=False
    )
```

```python
import functools

import jax
import jax.numpy as jnp
from jax import lax
from jax.experimental import pallas as pl
from jax.experimental.pallas import tpu as pltpu
from jax.sharding import Mesh
from jax.sharding import PartitionSpec as P

ADAPTER_SCALE = 2.0
X, CORES = 4, 2
DP, TENSOR = ("x", "y"), ("z", "core")
LANES = 128
WEIGHTS = (1, 1, 1, 50000, 1)
KERNEL_VMEM, COPIES_VMEM = 8 << 20, 60 << 20
PROJECT_VMEM, PROJECT_PARTS = 60 << 20, 2


def cost(flops, size):
    return pl.CostEstimate(flops=flops, bytes_accessed=2 * size, transcendentals=0)


def copies_kernel(down_ref, up_ref, out_ref, stage, ups, in_sems, sems):
    slots, rank, features = down_ref.shape
    packed = stage.shape[0] - slots * rank
    first = [
        pltpu.make_async_copy(down_ref.at[j], stage.at[pl.ds(j * rank, rank)], in_sems.at[j])
        for j in range(slots)
    ]
    first.append(pltpu.make_async_copy(up_ref, ups, in_sems.at[slots]))
    copies = [
        pltpu.make_async_copy(stage, out_ref.at[i], sems.at[i]) for i in range(out_ref.shape[0])
    ]
    for copy in first:
        copy.start()
    for copy in first:
        copy.wait()
    both = jnp.concatenate([ups[j] for j in range(slots)], axis=1)
    for q in range(features // LANES):
        block = both[q * packed : (q + 1) * packed]
        stage[slots * rank :, q * LANES : (q + 1) * LANES] = block
    for copy in copies:
        copy.start()
    for copy in copies:
        copy.wait()


def factor_copies(down, up, count):
    slots, rank, features = down.shape
    rows = slots * rank + rank * LANES // features
    return pl.pallas_call(
        copies_kernel,
        out_shape=jax.ShapeDtypeStruct((count, rows, features), down.dtype),
        in_specs=[pl.BlockSpec(memory_space=pl.ANY)] * 2,
        out_specs=pl.BlockSpec(memory_space=pl.ANY),
        scratch_shapes=[
            pltpu.VMEM((rows, features), down.dtype),
            pltpu.VMEM(up.shape, up.dtype),
            pltpu.SemaphoreType.DMA((slots + 1,)),
            pltpu.SemaphoreType.DMA((count,)),
        ],
        cost_estimate=cost(0, count * rows * features),
        compiler_params=pltpu.CompilerParams(vmem_limit_bytes=PROJECT_VMEM),
        name="factor_copies",
    )(down, up)


def project_kernel(hidden_ref, matrix_ref, *refs):
    *out_refs, mine, whole, chosen, stage, in_sems, out_sems = refs
    near_ref, middle_ref = out_refs[:2]
    span = middle_ref.shape[0] // 2
    columns = span // CORES
    chips = whole.shape[1] // span
    tokens = mine.shape[0]
    rows = tokens // PROJECT_PARTS

    take = [pltpu.make_async_copy(matrix_ref, whole, in_sems.at[0])] + [
        pltpu.make_async_copy(
            hidden_ref.at[pl.ds(i * rows, rows)], mine.at[pl.ds(i * rows, rows)], in_sems.at[1 + i]
        )
        for i in range(PROJECT_PARTS)
    ]
    for copy in take:
        copy.start()

    here = lax.axis_index("z")
    low = lax.broadcasted_iota(jnp.int32, (whole.shape[0], span), 1) < columns

    def block(chip):
        start = pl.multiple_of(lax.rem(chip + chips, chips) * span, span)
        return whole[:, pl.ds(start, span)]

    def turned(value):
        return jnp.concatenate([value[:, columns:], value[:, :columns]], axis=1)

    take[0].wait()
    for core, flip in enumerate((True, False)):
        upper = (lax.axis_index("core") == 1) != flip
        own, far = block(here), block(here + chips // 2)
        own = jnp.where(upper, turned(own), own)
        far = jnp.where(upper, far, turned(far))
        chosen[2 * core, :, :span] = block(here + jnp.where(upper, -3, 3))
        chosen[2 * core, :, span:] = jnp.where(low, own, far)
        chosen[2 * core + 1, :, :span] = block(here + jnp.where(upper, -2, 2))
        chosen[2 * core + 1, :, span:] = block(here + jnp.where(upper, -1, 1))

    places = [
        [(near_ref, 0)],
        [(middle_ref, 0)],
        [(out_refs[2], 0), (out_refs[5], span)],
        [(out_refs[3], 0), (out_refs[4], span)],
    ]
    leave = []
    for g, group in enumerate(places):
        for i in range(PROJECT_PARTS):
            if g == 0:
                take[1 + i].wait()
            part = slice(i * rows, (i + 1) * rows)
            product = jnp.dot(mine[part], chosen[g], preferred_element_type=jnp.float32)
            stage[g, :, part] = product.astype(stage.dtype).T
        for ref, start in group:
            copy = pltpu.make_async_copy(
                stage.at[g, pl.ds(start, ref.shape[0])], ref, out_sems.at[len(leave)]
            )
            copy.start()
            leave.append(copy)
    for copy in leave:
        copy.wait()


def project(hidden, matrix, columns):
    tokens, features = hidden.shape
    kind = hidden.dtype
    span = CORES * columns
    heights = [2 * span] * 2 + [span] * 4
    anywhere = pl.BlockSpec(memory_space=pl.ANY)
    return pl.pallas_call(
        project_kernel,
        out_shape=[jax.ShapeDtypeStruct((height, tokens), kind) for height in heights],
        in_specs=[anywhere] * 2,
        out_specs=[anywhere] * len(heights),
        scratch_shapes=[
            pltpu.VMEM(hidden.shape, kind),
            pltpu.VMEM(matrix.shape, kind),
            pltpu.VMEM((4, features, 2 * span), kind),
            pltpu.VMEM((4, 2 * span, tokens), kind),
            pltpu.SemaphoreType.DMA((1 + PROJECT_PARTS,)),
            pltpu.SemaphoreType.DMA((len(heights),)),
        ],
        cost_estimate=cost(0, 0),
        compiler_params=pltpu.CompilerParams(vmem_limit_bytes=PROJECT_VMEM),
        name="project",
    )(hidden, matrix)


def vmem_call(kernel, name, weight, out_shape, *operands):
    size = operands[0].size
    several = isinstance(out_shape, list)
    spec = pl.BlockSpec(memory_space=pltpu.VMEM)
    return pl.pallas_call(
        kernel,
        out_shape=out_shape,
        in_specs=[spec] * len(operands),
        out_specs=[spec] * len(out_shape) if several else spec,
        cost_estimate=cost(weight * size, 3 * size),
        compiler_params=pltpu.CompilerParams(vmem_limit_bytes=COPIES_VMEM if name == "add_parts" else KERNEL_VMEM),
        name=name,
    )(*operands)


def like(value, rows=None):
    return jax.ShapeDtypeStruct((rows or value.shape[0], *value.shape[1:]), value.dtype)


def sum_refs(*values):
    total = values[0].astype(jnp.float32)
    for value in values[1:]:
        total += value.astype(jnp.float32)
    return total.astype(values[0].dtype)


def add_kernel(first, part_ref, other_ref, came_ref, out_ref):
    other = other_ref[first : first + part_ref.shape[0]]
    out_ref[...] = sum_refs(part_ref[...], other, came_ref[...])


def add_far_kernel(first, tail_ref, other_ref, far_out_ref, own_out_ref):
    total = sum_refs(tail_ref[...], other_ref[first : first + tail_ref.shape[0]])
    columns = own_out_ref.shape[0]
    own_out_ref[...] = total[:columns]
    far_out_ref[...] = total[columns:]


def add_own_kernel(first, part_ref, other_ref, came_ref, out_ref):
    columns = came_ref.shape[0]
    core = lax.axis_index("core")
    mine = pl.ds(pl.multiple_of(core * columns, columns), columns)
    out_ref[...] = sum_refs(part_ref[...], other_ref[first : first + part_ref.shape[0]])
    out_ref[mine] = sum_refs(out_ref[mine], came_ref[...])


def split_kernel(own_ref, chain_ref, kept_ref, sent_ref):
    columns = own_ref.shape[0]
    core = lax.axis_index("core")
    mine = pl.ds(pl.multiple_of(core * columns, columns), columns)
    theirs = pl.ds(pl.multiple_of((1 - core) * columns, columns), columns)
    kept_ref[...] = sum_refs(own_ref[...], chain_ref[mine])
    sent_ref[...] = chain_ref[theirs]


def hop(value):
    n = lax.axis_size("z")
    pairs = [
        (z * CORES + core, (z + (1 - 2 * core)) % n * CORES + core)
        for z in range(n)
        for core in range(CORES)
    ]
    return lax.ppermute(value, TENSOR, pairs)


def along(axis, value, step):
    n = lax.axis_size(axis)
    return lax.ppermute(value, axis, [(i, (i + step) % n) for i in range(n)])


def pick_kernel(slots, rank, index_ref, row_ref, out_ref):
    dests, _, features = out_ref.shape
    packed = rank * LANES // features
    rollouts = index_ref.shape[0] // dests
    half = LANES // 2
    low = lax.broadcasted_iota(jnp.int32, (packed, LANES), 1) < half
    for d in range(dests):
        ups = []
        for r in range(rollouts):
            index = index_ref[d * rollouts + r]
            owner, place = index // slots, index % slots
            start = pl.multiple_of(place * rank, rank)
            out_ref[d, r * rank : (r + 1) * rank] = row_ref[owner, pl.ds(start, rank)]
            ups.append((row_ref[owner, slots * rank :], place))
        for p in range(rollouts // 2):
            for q in range(features // LANES):
                lanes = slice(q * LANES, (q + 1) * LANES)
                pair = []
                for h in range(2):
                    block, place = ups[2 * p + h]
                    block = block[:, lanes]
                    turned = jnp.concatenate([block[:, half:], block[:, :half]], axis=1)
                    pair.append(jnp.where(place == h, block, turned))
                at = rollouts * rank + p * packed
                out_ref[d, at : at + packed, lanes] = jnp.where(low, pair[0], pair[1])


def pick(index, row, dests, slots, rank):
    features = row.shape[2]
    packed = rank * LANES // features
    rollouts = index.shape[0] // dests
    rows = rollouts * rank + rollouts // 2 * packed
    return pl.pallas_call(
        functools.partial(pick_kernel, slots, rank),
        out_shape=jax.ShapeDtypeStruct((dests, rows, features), row.dtype),
        in_specs=[
            pl.BlockSpec(memory_space=pltpu.SMEM),
            pl.BlockSpec(memory_space=pltpu.VMEM),
        ],
        out_specs=pl.BlockSpec(memory_space=pltpu.VMEM),
        cost_estimate=cost(0, 2 * dests * rows * features),
        compiler_params=pltpu.CompilerParams(vmem_limit_bytes=KERNEL_VMEM),
        name="pick_factors",
    )(index, row)


def down_kernel(own_row_ref, hidden_ref, factor_ref, out_ref, up_ref):
    members, rank, chunk = out_ref.shape
    packed = up_ref.shape[1]
    count = own_row_ref.shape[0]
    per = members // count
    length = per * chunk
    for r in range(count):
        product = lax.dot_general(
            hidden_ref[r * length : (r + 1) * length],
            factor_ref[own_row_ref[r], r * rank : (r + 1) * rank],
            (((1,), (1,)), ((), ())),
            preferred_element_type=jnp.float32,
        ).T.astype(out_ref.dtype)
        for i in range(per):
            out_ref[r * per + i] = product[:, i * chunk : (i + 1) * chunk]
        at = count * rank + r // 2 * packed
        up_ref[r] = factor_ref[own_row_ref[r], at : at + packed]


def down_projection(own_row, hidden, factors, members, rank):
    tokens, features = hidden.shape
    packed = rank * LANES // features
    return pl.pallas_call(
        down_kernel,
        out_shape=[
            jax.ShapeDtypeStruct((members, rank, tokens // members), hidden.dtype),
            jax.ShapeDtypeStruct((own_row.shape[0], packed, features), factors.dtype),
        ],
        in_specs=[pl.BlockSpec(memory_space=pltpu.SMEM)]
        + [pl.BlockSpec(memory_space=pltpu.VMEM)] * 2,
        out_specs=[pl.BlockSpec(memory_space=pltpu.VMEM)] * 2,
        cost_estimate=cost(2 * tokens * features * rank, hidden.size + tokens * rank),
        compiler_params=pltpu.CompilerParams(vmem_limit_bytes=KERNEL_VMEM),
        name="down_projection",
    )(own_row, hidden, factors)


def sum_kernel(parts_ref, out_ref):
    total = parts_ref[0].astype(jnp.float32)
    for i in range(1, parts_ref.shape[0]):
        total += parts_ref[i].astype(jnp.float32)
    total = total.astype(out_ref.dtype)
    for i in range(out_ref.shape[0]):
        out_ref[i] = total


def sum_copies(parts):
    return pl.pallas_call(
        sum_kernel,
        out_shape=jax.ShapeDtypeStruct(parts.shape, parts.dtype),
        in_specs=[pl.BlockSpec(memory_space=pltpu.VMEM)],
        out_specs=pl.BlockSpec(memory_space=pltpu.VMEM),
        cost_estimate=cost(parts.size, 2 * parts.size),
        compiler_params=pltpu.CompilerParams(vmem_limit_bytes=KERNEL_VMEM),
        name="sum_parts",
    )(parts)


def final_kernel(lengths_ref, *refs):
    *base_refs, down_ref, up_ref, out_ref = refs
    columns, tokens = out_ref.shape
    members, rank, chunk = down_ref.shape
    count, _, features = up_ref.shape
    per, length = members // count, tokens // count
    for r in range(count):
        block = up_ref[r]
        first = r % 2 * columns
        up = jnp.concatenate(
            [
                block[:, q * LANES + first : q * LANES + first + columns]
                for q in range(features // LANES)
            ],
            axis=0,
        )
        down = jnp.concatenate([down_ref[r * per + i] for i in range(per)], axis=1)
        update = lax.dot_general(
            up, down, (((0,), (0,)), ((), ())), preferred_element_type=jnp.float32
        )
        span = slice(r * length, (r + 1) * length)
        total = ADAPTER_SCALE * update
        for base_ref in base_refs:
            total += base_ref[:, span].astype(jnp.float32)
        position = lax.broadcasted_iota(jnp.int32, (columns, length), 1)
        out_ref[:, span] = jnp.where(position < lengths_ref[r], total, 0.0).astype(out_ref.dtype)


def final(lengths, base, down, ups):
    columns, tokens = base[0].shape
    rank = down.shape[1]
    return pl.pallas_call(
        final_kernel,
        out_shape=jax.ShapeDtypeStruct(base[0].shape, base[0].dtype),
        in_specs=[pl.BlockSpec(memory_space=pltpu.SMEM)]
        + [pl.BlockSpec(memory_space=pltpu.VMEM)] * (len(base) + 2),
        out_specs=pl.BlockSpec(memory_space=pltpu.VMEM),
        cost_estimate=cost(2 * tokens * columns * rank, 4 * base[0].size + down.size),
        compiler_params=pltpu.CompilerParams(vmem_limit_bytes=KERNEL_VMEM),
        name="add_update",
    )(lengths, *base, down, ups)


def on_device(
    hidden, value_matrix, adapter_down_store, adapter_up_store, adapter_slot, rollout_adapter, lengths
):
    members = lax.axis_size(TENSOR)
    rollouts = rollout_adapter.shape[0]
    slots_here, rank, _ = adapter_up_store.shape
    row_slots = slots_here * lax.axis_size("y")

    copies = factor_copies(
        jnp.swapaxes(adapter_down_store, 1, 2), adapter_up_store, lax.axis_size("y")
    )
    row = lax.all_to_all(copies, "y", 0, 0)

    columns = adapter_up_store.shape[2]
    span = CORES * columns
    near, middle, *parts, tail = project(hidden, value_matrix, columns)
    near, middle = along("core", near, 1), along("core", middle, 1)
    *parts, tail, rollout_adapter = lax.optimization_barrier((*parts, tail, rollout_adapter))

    def add(kernel, first, weight, name, part, *others):
        return vmem_call(functools.partial(kernel, first), name, weight, like(part), part, *others)

    chain, own = vmem_call(
        functools.partial(add_far_kernel, span),
        "add_far",
        WEIGHTS[0],
        [like(tail, columns)] * 2,
        tail,
        near,
    )
    chain = add(add_own_kernel, 0, WEIGHTS[1], "add_own", parts[0], near, hop(chain))
    chain = add(add_kernel, 0, WEIGHTS[2], "add_parts", parts[1], middle, hop(chain))
    chain = add(add_kernel, span, WEIGHTS[3], "add_parts", parts[2], middle, hop(chain))
    kept, sent = vmem_call(
        split_kernel, "split", WEIGHTS[4], [like(own), like(own)], own, hop(chain)
    )
    base = (kept, along("core", sent, 1))

    here = lax.axis_index("x")
    mine = jnp.arange(X, dtype=jnp.int32)[:, None] == here
    wanted = lax.psum(jnp.where(mine, rollout_adapter[None, :], 0), "x").reshape(-1)
    table = jnp.arange(adapter_slot.shape[0], dtype=jnp.int32)
    matches = wanted[:, None] == table[None, :]
    slots = jnp.sum(jnp.where(matches, adapter_slot[None, :], 0), axis=1)
    local = jnp.clip(slots - here * row_slots, 0, row_slots - 1)
    own_row = lax.dynamic_slice_in_dim(slots, here * rollouts, rollouts) // row_slots
    local, own_row = lax.optimization_barrier((local, own_row))

    sent = pick(local, row, X, slots_here, rank)
    factors = lax.all_to_all(sent, "x", 0, 0)
    down, ups = down_projection(own_row, hidden, factors, members, rank)
    down = lax.all_to_all(down, TENSOR, 0, 0)
    down = sum_copies(down)
    down = lax.all_to_all(down, TENSOR, 0, 0)
    return final(lengths, base, down, ups).T


def solution(mesh):
    dp, tensor = mesh.devices.shape
    fine = Mesh(mesh.devices.reshape(X, dp // X, tensor // CORES, CORES), (*DP, *TENSOR))
    in_specs = (
        P(DP, TENSOR),
        P(TENSOR, None),
        P(DP, TENSOR, None),
        P(DP, None, TENSOR),
        P(),
        P(DP),
        P(DP),
    )
    return jax.shard_map(
        on_device, mesh=fine, in_specs=in_specs, out_specs=P(DP, TENSOR), check_vma=False
    )
```

```python
import functools

import jax
import jax.numpy as jnp
from jax import lax
from jax.experimental import pallas as pl
from jax.experimental.pallas import tpu as pltpu
from jax.sharding import Mesh
from jax.sharding import PartitionSpec as P

ADAPTER_SCALE = 2.0
X, CORES = 4, 2
DP, TENSOR = ("x", "y"), ("z", "core")
LANES = 128
WEIGHTS = (1, 1, 1, 50000, 1)
KERNEL_VMEM, COPIES_VMEM = 8 << 20, 60 << 20
PROJECT_VMEM, PROJECT_PARTS = 60 << 20, 2


def cost(flops, size):
    return pl.CostEstimate(flops=flops, bytes_accessed=2 * size, transcendentals=0)


def copies_kernel(down_ref, up_ref, out_ref, stage, ups, in_sems, sems):
    slots, rank, features = down_ref.shape
    packed = stage.shape[0] - slots * rank
    first = [
        pltpu.make_async_copy(down_ref.at[j], stage.at[pl.ds(j * rank, rank)], in_sems.at[j])
        for j in range(slots)
    ]
    first.append(pltpu.make_async_copy(up_ref, ups, in_sems.at[slots]))
    copies = [
        pltpu.make_async_copy(stage, out_ref.at[i], sems.at[i]) for i in range(out_ref.shape[0])
    ]
    for copy in first:
        copy.start()
    for copy in first:
        copy.wait()
    both = jnp.concatenate([ups[j] for j in range(slots)], axis=1)
    for q in range(features // LANES):
        block = both[q * packed : (q + 1) * packed]
        stage[slots * rank :, q * LANES : (q + 1) * LANES] = block
    for copy in copies:
        copy.start()
    for copy in copies:
        copy.wait()


def factor_copies(down, up, count):
    slots, rank, features = down.shape
    rows = slots * rank + rank * LANES // features
    return pl.pallas_call(
        copies_kernel,
        out_shape=jax.ShapeDtypeStruct((count, rows, features), down.dtype),
        in_specs=[pl.BlockSpec(memory_space=pl.ANY)] * 2,
        out_specs=pl.BlockSpec(memory_space=pl.ANY),
        scratch_shapes=[
            pltpu.VMEM((rows, features), down.dtype),
            pltpu.VMEM(up.shape, up.dtype),
            pltpu.SemaphoreType.DMA((slots + 1,)),
            pltpu.SemaphoreType.DMA((count,)),
        ],
        cost_estimate=cost(0, count * rows * features),
        compiler_params=pltpu.CompilerParams(vmem_limit_bytes=PROJECT_VMEM),
        name="factor_copies",
    )(down, up)


def project_kernel(hidden_ref, matrix_ref, *refs):
    *out_refs, mine, whole, chosen, stage, in_sems, out_sems = refs
    near_ref, middle_ref = out_refs[:2]
    span = middle_ref.shape[0] // 2
    columns = span // CORES
    chips = whole.shape[1] // span
    tokens = mine.shape[0]
    rows = tokens // PROJECT_PARTS

    take = [pltpu.make_async_copy(matrix_ref, whole, in_sems.at[0])] + [
        pltpu.make_async_copy(
            hidden_ref.at[pl.ds(i * rows, rows)], mine.at[pl.ds(i * rows, rows)], in_sems.at[1 + i]
        )
        for i in range(PROJECT_PARTS)
    ]
    for copy in take:
        copy.start()

    here = lax.axis_index("z")
    low = lax.broadcasted_iota(jnp.int32, (whole.shape[0], span), 1) < columns

    def block(chip):
        start = pl.multiple_of(lax.rem(chip + chips, chips) * span, span)
        return whole[:, pl.ds(start, span)]

    def turned(value):
        return jnp.concatenate([value[:, columns:], value[:, :columns]], axis=1)

    take[0].wait()
    for core, flip in enumerate((True, False)):
        upper = (lax.axis_index("core") == 1) != flip
        own, far = block(here), block(here + chips // 2)
        own = jnp.where(upper, turned(own), own)
        far = jnp.where(upper, far, turned(far))
        chosen[2 * core, :, :span] = block(here + jnp.where(upper, -3, 3))
        chosen[2 * core, :, span:] = jnp.where(low, own, far)
        chosen[2 * core + 1, :, :span] = block(here + jnp.where(upper, -2, 2))
        chosen[2 * core + 1, :, span:] = block(here + jnp.where(upper, -1, 1))

    places = [
        [(near_ref, 0)],
        [(middle_ref, 0)],
        [(out_refs[2], 0), (out_refs[5], span)],
        [(out_refs[3], 0), (out_refs[4], span)],
    ]
    leave = []
    for g, group in enumerate(places):
        for i in range(PROJECT_PARTS):
            if g == 0:
                take[1 + i].wait()
            part = slice(i * rows, (i + 1) * rows)
            product = jnp.dot(mine[part], chosen[g], preferred_element_type=jnp.float32)
            stage[g, :, part] = product.astype(stage.dtype).T
            span_of = pl.ds(i * rows, rows)
            for ref, start in group:
                copy = pltpu.make_async_copy(
                    stage.at[g, pl.ds(start, ref.shape[0]), span_of],
                    ref.at[:, span_of],
                    out_sems.at[len(leave)],
                )
                copy.start()
                leave.append(copy)
    for copy in leave:
        copy.wait()


def project(hidden, matrix, columns):
    tokens, features = hidden.shape
    kind = hidden.dtype
    span = CORES * columns
    heights = [2 * span] * 2 + [span] * 4
    anywhere = pl.BlockSpec(memory_space=pl.ANY)
    return pl.pallas_call(
        project_kernel,
        out_shape=[jax.ShapeDtypeStruct((height, tokens), kind) for height in heights],
        in_specs=[anywhere] * 2,
        out_specs=[anywhere] * len(heights),
        scratch_shapes=[
            pltpu.VMEM(hidden.shape, kind),
            pltpu.VMEM(matrix.shape, kind),
            pltpu.VMEM((4, features, 2 * span), kind),
            pltpu.VMEM((4, 2 * span, tokens), kind),
            pltpu.SemaphoreType.DMA((1 + PROJECT_PARTS,)),
            pltpu.SemaphoreType.DMA((len(heights) * PROJECT_PARTS,)),
        ],
        cost_estimate=cost(0, 0),
        compiler_params=pltpu.CompilerParams(vmem_limit_bytes=PROJECT_VMEM),
        name="project",
    )(hidden, matrix)


def vmem_call(kernel, name, weight, out_shape, *operands):
    size = operands[0].size
    several = isinstance(out_shape, list)
    spec = pl.BlockSpec(memory_space=pltpu.VMEM)
    return pl.pallas_call(
        kernel,
        out_shape=out_shape,
        in_specs=[spec] * len(operands),
        out_specs=[spec] * len(out_shape) if several else spec,
        cost_estimate=cost(weight * size, 3 * size),
        compiler_params=pltpu.CompilerParams(vmem_limit_bytes=COPIES_VMEM if name == "add_parts" else KERNEL_VMEM),
        name=name,
    )(*operands)


def like(value, rows=None):
    return jax.ShapeDtypeStruct((rows or value.shape[0], *value.shape[1:]), value.dtype)


def sum_refs(*values):
    total = values[0].astype(jnp.float32)
    for value in values[1:]:
        total += value.astype(jnp.float32)
    return total.astype(values[0].dtype)


def add_kernel(first, part_ref, other_ref, came_ref, out_ref):
    other = other_ref[first : first + part_ref.shape[0]]
    out_ref[...] = sum_refs(part_ref[...], other, came_ref[...])


def add_far_kernel(first, tail_ref, other_ref, far_out_ref, own_out_ref):
    total = sum_refs(tail_ref[...], other_ref[first : first + tail_ref.shape[0]])
    columns = own_out_ref.shape[0]
    own_out_ref[...] = total[:columns]
    far_out_ref[...] = total[columns:]


def add_own_kernel(first, part_ref, other_ref, came_ref, out_ref):
    columns = came_ref.shape[0]
    core = lax.axis_index("core")
    mine = pl.ds(pl.multiple_of(core * columns, columns), columns)
    out_ref[...] = sum_refs(part_ref[...], other_ref[first : first + part_ref.shape[0]])
    out_ref[mine] = sum_refs(out_ref[mine], came_ref[...])


def split_kernel(own_ref, chain_ref, kept_ref, sent_ref):
    columns = own_ref.shape[0]
    core = lax.axis_index("core")
    mine = pl.ds(pl.multiple_of(core * columns, columns), columns)
    theirs = pl.ds(pl.multiple_of((1 - core) * columns, columns), columns)
    kept_ref[...] = sum_refs(own_ref[...], chain_ref[mine])
    sent_ref[...] = chain_ref[theirs]


def hop(value):
    n = lax.axis_size("z")
    pairs = [
        (z * CORES + core, (z + (1 - 2 * core)) % n * CORES + core)
        for z in range(n)
        for core in range(CORES)
    ]
    return lax.ppermute(value, TENSOR, pairs)


def along(axis, value, step):
    n = lax.axis_size(axis)
    return lax.ppermute(value, axis, [(i, (i + step) % n) for i in range(n)])


def pick_kernel(slots, rank, index_ref, row_ref, out_ref):
    dests, _, features = out_ref.shape
    packed = rank * LANES // features
    rollouts = index_ref.shape[0] // dests
    half = LANES // 2
    low = lax.broadcasted_iota(jnp.int32, (packed, LANES), 1) < half
    for d in range(dests):
        ups = []
        for r in range(rollouts):
            index = index_ref[d * rollouts + r]
            owner, place = index // slots, index % slots
            start = pl.multiple_of(place * rank, rank)
            out_ref[d, r * rank : (r + 1) * rank] = row_ref[owner, pl.ds(start, rank)]
            ups.append((row_ref[owner, slots * rank :], place))
        for p in range(rollouts // 2):
            for q in range(features // LANES):
                lanes = slice(q * LANES, (q + 1) * LANES)
                pair = []
                for h in range(2):
                    block, place = ups[2 * p + h]
                    block = block[:, lanes]
                    turned = jnp.concatenate([block[:, half:], block[:, :half]], axis=1)
                    pair.append(jnp.where(place == h, block, turned))
                at = rollouts * rank + p * packed
                out_ref[d, at : at + packed, lanes] = jnp.where(low, pair[0], pair[1])


def pick(index, row, dests, slots, rank):
    features = row.shape[2]
    packed = rank * LANES // features
    rollouts = index.shape[0] // dests
    rows = rollouts * rank + rollouts // 2 * packed
    return pl.pallas_call(
        functools.partial(pick_kernel, slots, rank),
        out_shape=jax.ShapeDtypeStruct((dests, rows, features), row.dtype),
        in_specs=[
            pl.BlockSpec(memory_space=pltpu.SMEM),
            pl.BlockSpec(memory_space=pltpu.VMEM),
        ],
        out_specs=pl.BlockSpec(memory_space=pltpu.VMEM),
        cost_estimate=cost(0, 2 * dests * rows * features),
        compiler_params=pltpu.CompilerParams(vmem_limit_bytes=KERNEL_VMEM),
        name="pick_factors",
    )(index, row)


def down_kernel(own_row_ref, hidden_ref, factor_ref, out_ref, up_ref):
    members, rank, chunk = out_ref.shape
    packed = up_ref.shape[1]
    count = own_row_ref.shape[0]
    per = members // count
    length = per * chunk
    for r in range(count):
        product = lax.dot_general(
            hidden_ref[r * length : (r + 1) * length],
            factor_ref[own_row_ref[r], r * rank : (r + 1) * rank],
            (((1,), (1,)), ((), ())),
            preferred_element_type=jnp.float32,
        ).T.astype(out_ref.dtype)
        for i in range(per):
            out_ref[r * per + i] = product[:, i * chunk : (i + 1) * chunk]
        at = count * rank + r // 2 * packed
        up_ref[r] = factor_ref[own_row_ref[r], at : at + packed]


def down_projection(own_row, hidden, factors, members, rank):
    tokens, features = hidden.shape
    packed = rank * LANES // features
    return pl.pallas_call(
        down_kernel,
        out_shape=[
            jax.ShapeDtypeStruct((members, rank, tokens // members), hidden.dtype),
            jax.ShapeDtypeStruct((own_row.shape[0], packed, features), factors.dtype),
        ],
        in_specs=[pl.BlockSpec(memory_space=pltpu.SMEM)]
        + [pl.BlockSpec(memory_space=pltpu.VMEM)] * 2,
        out_specs=[pl.BlockSpec(memory_space=pltpu.VMEM)] * 2,
        cost_estimate=cost(2 * tokens * features * rank, hidden.size + tokens * rank),
        compiler_params=pltpu.CompilerParams(vmem_limit_bytes=KERNEL_VMEM),
        name="down_projection",
    )(own_row, hidden, factors)


def sum_kernel(parts_ref, out_ref):
    total = parts_ref[0].astype(jnp.float32)
    for i in range(1, parts_ref.shape[0]):
        total += parts_ref[i].astype(jnp.float32)
    total = total.astype(out_ref.dtype)
    for i in range(out_ref.shape[0]):
        out_ref[i] = total


def sum_copies(parts):
    return pl.pallas_call(
        sum_kernel,
        out_shape=jax.ShapeDtypeStruct(parts.shape, parts.dtype),
        in_specs=[pl.BlockSpec(memory_space=pltpu.VMEM)],
        out_specs=pl.BlockSpec(memory_space=pltpu.VMEM),
        cost_estimate=cost(parts.size, 2 * parts.size),
        compiler_params=pltpu.CompilerParams(vmem_limit_bytes=KERNEL_VMEM),
        name="sum_parts",
    )(parts)


def final_kernel(lengths_ref, *refs):
    *base_refs, down_ref, up_ref, out_ref = refs
    columns, tokens = out_ref.shape
    members, rank, chunk = down_ref.shape
    count, _, features = up_ref.shape
    per, length = members // count, tokens // count
    for r in range(count):
        block = up_ref[r]
        first = r % 2 * columns
        up = jnp.concatenate(
            [
                block[:, q * LANES + first : q * LANES + first + columns]
                for q in range(features // LANES)
            ],
            axis=0,
        )
        down = jnp.concatenate([down_ref[r * per + i] for i in range(per)], axis=1)
        update = lax.dot_general(
            up, down, (((0,), (0,)), ((), ())), preferred_element_type=jnp.float32
        )
        span = slice(r * length, (r + 1) * length)
        total = ADAPTER_SCALE * update
        for base_ref in base_refs:
            total += base_ref[:, span].astype(jnp.float32)
        position = lax.broadcasted_iota(jnp.int32, (columns, length), 1)
        out_ref[:, span] = jnp.where(position < lengths_ref[r], total, 0.0).astype(out_ref.dtype)


def final(lengths, base, down, ups):
    columns, tokens = base[0].shape
    rank = down.shape[1]
    return pl.pallas_call(
        final_kernel,
        out_shape=jax.ShapeDtypeStruct(base[0].shape, base[0].dtype),
        in_specs=[pl.BlockSpec(memory_space=pltpu.SMEM)]
        + [pl.BlockSpec(memory_space=pltpu.VMEM)] * (len(base) + 2),
        out_specs=pl.BlockSpec(memory_space=pltpu.VMEM),
        cost_estimate=cost(2 * tokens * columns * rank, 4 * base[0].size + down.size),
        compiler_params=pltpu.CompilerParams(vmem_limit_bytes=KERNEL_VMEM),
        name="add_update",
    )(lengths, *base, down, ups)


def on_device(
    hidden, value_matrix, adapter_down_store, adapter_up_store, adapter_slot, rollout_adapter, lengths
):
    members = lax.axis_size(TENSOR)
    rollouts = rollout_adapter.shape[0]
    slots_here, rank, _ = adapter_up_store.shape
    row_slots = slots_here * lax.axis_size("y")

    copies = factor_copies(
        jnp.swapaxes(adapter_down_store, 1, 2), adapter_up_store, lax.axis_size("y")
    )
    row = lax.all_to_all(copies, "y", 0, 0)

    columns = adapter_up_store.shape[2]
    span = CORES * columns
    near, middle, *parts, tail = project(hidden, value_matrix, columns)
    near, middle = along("core", near, 1), along("core", middle, 1)
    *parts, tail, rollout_adapter = lax.optimization_barrier((*parts, tail, rollout_adapter))

    def add(kernel, first, weight, name, part, *others):
        return vmem_call(functools.partial(kernel, first), name, weight, like(part), part, *others)

    chain, own = vmem_call(
        functools.partial(add_far_kernel, span),
        "add_far",
        WEIGHTS[0],
        [like(tail, columns)] * 2,
        tail,
        near,
    )
    chain = add(add_own_kernel, 0, WEIGHTS[1], "add_own", parts[0], near, hop(chain))
    chain = add(add_kernel, 0, WEIGHTS[2], "add_parts", parts[1], middle, hop(chain))
    chain = add(add_kernel, span, WEIGHTS[3], "add_parts", parts[2], middle, hop(chain))
    kept, sent = vmem_call(
        split_kernel, "split", WEIGHTS[4], [like(own), like(own)], own, hop(chain)
    )
    base = (kept, along("core", sent, 1))

    here = lax.axis_index("x")
    mine = jnp.arange(X, dtype=jnp.int32)[:, None] == here
    wanted = lax.psum(jnp.where(mine, rollout_adapter[None, :], 0), "x").reshape(-1)
    table = jnp.arange(adapter_slot.shape[0], dtype=jnp.int32)
    matches = wanted[:, None] == table[None, :]
    slots = jnp.sum(jnp.where(matches, adapter_slot[None, :], 0), axis=1)
    local = jnp.clip(slots - here * row_slots, 0, row_slots - 1)
    own_row = lax.dynamic_slice_in_dim(slots, here * rollouts, rollouts) // row_slots
    local, own_row = lax.optimization_barrier((local, own_row))

    sent = pick(local, row, X, slots_here, rank)
    factors = lax.all_to_all(sent, "x", 0, 0)
    down, ups = down_projection(own_row, hidden, factors, members, rank)
    down = lax.all_to_all(down, TENSOR, 0, 0)
    down = sum_copies(down)
    down = lax.all_to_all(down, TENSOR, 0, 0)
    return final(lengths, base, down, ups).T


def solution(mesh):
    dp, tensor = mesh.devices.shape
    fine = Mesh(mesh.devices.reshape(X, dp // X, tensor // CORES, CORES), (*DP, *TENSOR))
    in_specs = (
        P(DP, TENSOR),
        P(TENSOR, None),
        P(DP, TENSOR, None),
        P(DP, None, TENSOR),
        P(),
        P(DP),
        P(DP),
    )
    return jax.shard_map(
        on_device, mesh=fine, in_specs=in_specs, out_specs=P(DP, TENSOR), check_vma=False
    )
```
